256 devices in a mesh: row: 16 (over z_lo, x, core), col: 16 (over z_hi, y).
Axes of the slice: x: 4, y: 4, z: 8 (z_hi: 4, z_lo: 2; z = z_hi * 2 + z_lo), core: 2. Of those that a mesh axis runs over, the one named last changes fastest.
Arguments:
- near: float32 [32, 32, 3, 3, 256, 256], P('row', 'col'), may hold values from -0.01 to 3.7
- interp: float32 [32, 32, 160, 160], P('row', 'col'), may hold values from -0.5 to 0.5
- red_count: int32 [32, 32], P('row', 'col'), may hold values from 96 to 160
- owner_flip: int32 [16, 16, 2], P('row', 'col'), may hold values from 0 to 1, as said below
Outputs:
- parents: float32 [16, 16, 640, 640], P('row', 'col')
The draws below stay inside these ranges and needn't reach their ends.
Inputs may be any that keep to these rules, and one draw needn't show every extreme that they name: owner_flip[i, j, :] is the same on the four devices of each aligned 2 x 2 group, rows 2 i and 2 i + 1, columns 2 j and 2 j + 1.
All inputs are finite; a program needn't handle non-finite values.
Results may differ from the reference program's by a relative error of at most 0.0001.
Values sent between devices are 32-bit elements; how exact they have to be, the bound alone decides.
No kernel may reach another device: no remote copies, remote signals or barrier semaphores. Data moves between devices by JAX's collectives and lax.ppermute only.
A program may use at most 128 MiB of HBM per device.

```python
import math
import jax
import jax.numpy as jnp
from jax import lax

PTS = 256
SLOTS = 160
LOW = 96
BR = 32
BC = 32
N_ROW = 16
N_COL = 16


FORWARD = ((0, 1), (1, -1), (1, 0), (1, 1))


def draw_near(key, part):
    offsets = jax.random.uniform(jax.random.fold_in(key, 101), (BR, BC, 2, PTS), jnp.float32)
    coefficient = jnp.exp(jax.random.uniform(jax.random.fold_in(key, 102), (BR, BC, PTS), jnp.float32, math.log(0.2), math.log(0.6)))
    diag_values = jax.random.uniform(jax.random.fold_in(key, 103), (BR, BC, PTS), jnp.float32, 1.0, 2.0)
    row_places = jnp.arange(BR, dtype=jnp.int32).astype(jnp.float32)
    col_places = jnp.arange(BC, dtype=jnp.int32).astype(jnp.float32)
    pos_x = row_places[:, None, None] + offsets[:, :, 0, :]
    pos_y = col_places[None, :, None] + offsets[:, :, 1, :]
    pad_x = jnp.pad(pos_x, ((1, 1), (1, 1), (0, 0)))
    pad_y = jnp.pad(pos_y, ((1, 1), (1, 1), (0, 0)))
    pad_coef = jnp.pad(coefficient, ((1, 1), (1, 1), (0, 0)))
    identity = jnp.eye(PTS, dtype=jnp.float32)
    store = jnp.zeros((BR, BC, 3, 3, PTS, PTS), jnp.float32)
    for row_step in (-1, 0, 1):
        for col_step in (-1, 0, 1):
            other_x = pad_x[1 + row_step:1 + row_step + BR, 1 + col_step:1 + col_step + BC]
            other_y = pad_y[1 + row_step:1 + row_step + BR, 1 + col_step:1 + col_step + BC]
            other_coef = pad_coef[1 + row_step:1 + row_step + BR, 1 + col_step:1 + col_step + BC]
            delta_x = pos_x[:, :, :, None] - other_x[:, :, None, :]
            delta_y = pos_y[:, :, :, None] - other_y[:, :, None, :]
            distance = jnp.sqrt(delta_x * delta_x + delta_y * delta_y)
            block = coefficient[:, :, :, None] * other_coef[:, :, None, :] * jnp.exp(-distance / 0.5)
            if row_step == 0 and col_step == 0:
                block = block + identity * diag_values[:, :, :, None]
            store = store.at[:, :, row_step + 1, col_step + 1].set(block)
    valid = jnp.pad(jnp.ones((BR, BC), jnp.float32), ((1, 1), (1, 1)))
    for number, (row_step, col_step) in enumerate(FORWARD):
        rough = jax.random.uniform(jax.random.fold_in(key, 110 + number), (BR, BC, PTS, PTS), jnp.float32, -0.01, 0.01)
        valid_here = valid[1 + row_step:1 + row_step + BR, 1 + col_step:1 + col_step + BC]
        rough = rough * valid_here[:, :, None, None]
        store = store.at[:, :, 1 + row_step, 1 + col_step].add(rough)
        padded_rough = jnp.pad(rough, ((1, 1), (1, 1), (0, 0), (0, 0)))
        behind = padded_rough[1 - row_step:1 - row_step + BR, 1 - col_step:1 - col_step + BC]
        store = store.at[:, :, 1 - row_step, 1 - col_step].add(jnp.swapaxes(behind, 2, 3))
    rough_centre = jax.random.uniform(jax.random.fold_in(key, 120), (BR, BC, PTS, PTS), jnp.float32, -0.01, 0.01)
    store = store.at[:, :, 1, 1].add(0.5 * (rough_centre + jnp.swapaxes(rough_centre, 2, 3)))
    return store


def draw_red_count(key, part):
    base_counts = jax.random.randint(jax.random.fold_in(key, 201), (BR * BC,), PTS - SLOTS, SLOTS + 1)
    shuffled = jax.random.permutation(jax.random.fold_in(key, 202), BR * BC)
    base_counts = base_counts.at[shuffled[0]].set(PTS - SLOTS)
    base_counts = base_counts.at[shuffled[1]].set(SLOTS)
    return base_counts.reshape(BR, BC).astype(jnp.int32)


def draw_owner_flip(key, part):
    groups = jax.random.randint(jax.random.fold_in(key, 301), (BR // 4 * (BC // 4), 2), 0, 2)
    groups = groups.at[0].set(jnp.array([0, 1], dtype=jnp.int32))
    groups = groups.at[1].set(jnp.array([1, 0], dtype=jnp.int32))
    groups = groups.reshape(BR // 4, BC // 4, 2)
    spread = jnp.repeat(jnp.repeat(groups, 2, axis=0), 2, axis=1)
    return spread.astype(jnp.int32)


def block_scale(key, shape, pieces, low, high):
    def one(axis_at, shards_of):
        draws = jax.random.uniform(jax.random.fold_in(jax.random.fold_in(key, 6), axis_at), (shards_of,), jnp.float32, low / len(pieces), high / len(pieces))
        return jnp.repeat(jnp.exp(draws), shape[axis_at] // shards_of).reshape((-1,) + (1,) * (len(shape) - axis_at - 1))

    loudness = one(*pieces[0])
    for cut in pieces[1:]:
        loudness = loudness * one(*cut)
    return loudness


def normal_values(stream_key, dims, width, most, pieces=(), kind=jnp.bfloat16):
    values = width * jax.random.normal(stream_key, dims, jnp.float32)
    if pieces:
        values = values * block_scale(stream_key, dims, pieces, -0.22, 0.18)
    return jnp.clip(values, -most, most).astype(kind)


def setup_inputs(seed: int = 0) -> dict:
    key_list = jax.random.split(jax.random.key(seed), 5)
    near = draw_near(jax.random.fold_in(key_list[4], 71), 0)
    interp = normal_values(key_list[1], (BR, BC, SLOTS, SLOTS), 0.08, 0.5, ((0, 16), (1, 16)), jnp.float32)
    red_count = draw_red_count(jax.random.fold_in(key_list[4], 71), 0)
    owner_flip = draw_owner_flip(jax.random.fold_in(key_list[4], 71), 0)
    return {"near": near, "interp": interp, "red_count": red_count, "owner_flip": owner_flip}


COLOURS = ((0, 0), (0, 1), (1, 0), (1, 1))
STEPS = (-1, 0, 1)
PRECISE = lax.Precision.HIGHEST

def reference(near, interp, red_count, owner_flip):
    store = jnp.pad(near, ((1, 1), (1, 1), (0, 0), (0, 0), (0, 0), (0, 0)))
    slot_index = jnp.arange(SLOTS, dtype=jnp.int32)
    point_index = jnp.arange(PTS, dtype=jnp.int32)
    identity = jnp.eye(SLOTS, dtype=jnp.float32)
    for colour, (home_row, home_col) in enumerate(COLOURS):
        blocks = store[1 + home_row:1 + home_row + BR:2, 1 + home_col:1 + home_col + BC:2]
        red_here = red_count[home_row::2, home_col::2]
        mask_red = (slot_index[None, None, :] < red_here[:, :, None]).astype(jnp.float32)
        mask_skel = (slot_index[None, None, :] + LOW >= red_here[:, :, None]).astype(jnp.float32)
        interp_masked = interp[home_row::2, home_col::2] * mask_red[:, :, :, None] * mask_skel[:, :, None, :]
        reduced = blocks[:, :, :, :, :SLOTS, :] - jnp.einsum('ijrs,ijabst->ijabrt', interp_masked, blocks[:, :, :, :, LOW:, :], precision=PRECISE)
        active_rows = []
        for row_step in STEPS:
            line_list = []
            for col_step in STEPS:
                if row_step == 0 and col_step == 0:
                    active_here = point_index[None, None, :] >= red_here[:, :, None]
                else:
                    active_here = jnp.ones((N_ROW, N_COL, PTS), dtype=bool)
                line_list.append(active_here.astype(jnp.float32))
            active_rows.append(jnp.stack(line_list, axis=2))
        active = jnp.stack(active_rows, axis=2)
        inner_rows = reduced * mask_red[:, :, None, None, :, None] * active[:, :, :, :, None, :]
        centre = reduced[:, :, 1, 1]
        red_block = centre[:, :, :, :SLOTS] - jnp.einsum('ijrt,ijqt->ijrq', centre[:, :, :, LOW:], interp_masked, precision=PRECISE)
        both_masks = mask_red[:, :, :, None] * mask_red[:, :, None, :]
        padded = jnp.where(both_masks > 0, red_block, identity)
        lower_factor = jnp.linalg.cholesky(padded)
        stacked = inner_rows.transpose(0, 1, 4, 2, 3, 5).reshape(N_ROW, N_COL, SLOTS, 9 * PTS)
        solved = jax.scipy.linalg.solve_triangular(lower_factor, stacked, lower=True)
        panels = solved.reshape(N_ROW, N_COL, SLOTS, 3, 3, PTS)
        for row_first in STEPS:
            for col_first in STEPS:
                row_low = max(row_first - 1, -1)
                row_high = min(row_first + 1, 1)
                col_low = max(col_first - 1, -1)
                col_high = min(col_first + 1, 1)
                single = panels[:, :, :, row_first + 1, col_first + 1, :]
                paired = panels[:, :, :, row_low + 1:row_high + 2, col_low + 1:col_high + 2, :]
                update = jnp.einsum('ijrc,ijrabd->ijabcd', single, paired, precision=PRECISE)
                target_row = 1 + home_row + row_first
                target_col = 1 + home_col + col_first
                store = store.at[target_row:target_row + BR:2, target_col:target_col + BC:2, row_low - row_first + 1:row_high - row_first + 2, col_low - col_first + 1:col_high - col_first + 2].add(-update)
    inner_store = store[1:1 + BR, 1:1 + BC]
    mask_child = (slot_index[None, None, :] + LOW >= red_count[:, :, None]).astype(jnp.float32)
    row_blocks = []
    for first_row, first_col in COLOURS:
        line_list = []
        for second_row, second_col in COLOURS:
            piece_block = inner_store[first_row::2, first_col::2, second_row - first_row + 1, second_col - first_col + 1, LOW:, LOW:]
            piece_block = piece_block * mask_child[first_row::2, first_col::2][:, :, :, None] * mask_child[second_row::2, second_col::2][:, :, None, :]
            line_list.append(piece_block)
        row_blocks.append(jnp.concatenate(line_list, axis=3))
    parent = jnp.concatenate(row_blocks, axis=2)
    device_rows = jnp.arange(N_ROW, dtype=jnp.int32)
    device_cols = jnp.arange(N_COL, dtype=jnp.int32)
    partner_rows = device_rows + 1 - 2 * (device_rows % 2)
    partner_cols = device_cols + 1 - 2 * (device_cols % 2)
    source_rows = jnp.where(owner_flip[:, :, 0] == 1, partner_rows[:, None], device_rows[:, None])
    source_cols = jnp.where(owner_flip[:, :, 1] == 1, partner_cols[None, :], device_cols[None, :])
    return parent[source_rows, source_cols]
```

```python
import functools

import jax
import jax.numpy as jnp
from jax import lax
from jax.experimental import pallas as pl
from jax.experimental.pallas import tpu as pltpu
from jax.sharding import PartitionSpec as P

BOXES = ((0, 0), (0, 1), (1, 0), (1, 1))
PTS = 256
SLOTS = 160
LOW = 96
GROUPS = SLOTS // 8
VMEM_LIMIT = 48 * 2**20
F32 = jnp.float32
BF16 = jnp.bfloat16
NN = (((1,), (0,)), ((), ()))
NT = (((1,), (1,)), ((), ()))
TN = (((0,), (0,)), ((), ()))


def near_each_other(a, b):
    return abs(a[0] - b[0]) <= 1 and abs(a[1] - b[1]) <= 1


def offsets_of(colour):
    row, col = BOXES[colour]
    step_row, step_col = 1 - 2 * row, 1 - 2 * col
    return ((0, 0), (0, step_col), (step_row, 0), (step_row, step_col))


def sources_of(colour):
    row, col = BOXES[colour]
    return [(row + 2 * dr, col + 2 * dc) for dr, dc in offsets_of(colour)]


def children_of(box):
    return [m for m in range(4) if near_each_other(BOXES[m], box)]


def moved(box, offset):
    return (box[0] - 2 * offset[0], box[1] - 2 * offset[1])


def pairs_of(colour):
    return [(b, m) for b in sources_of(colour) for m in children_of(b)]


def later_boxes(colour):
    return list(range(colour + 1, 4))


def local_keys(colour):
    return [
        (b, BOXES[n]) for n in later_boxes(colour) for b in sources_of(colour)
        if near_each_other(b, BOXES[n])
    ]


def update_terms(colour):
    terms = []
    for later in later_boxes(colour):
        for place, box in enumerate(sources_of(later)):
            for m in children_of(box):
                for b in sources_of(colour):
                    if near_each_other(b, box) and near_each_other(b, BOXES[m]):
                        terms.append((later, place, m, b, box))
    return terms


def remote_keys(colour):
    found = {}
    for later, place, m, b, box in update_terms(colour):
        offset = offsets_of(later)[place]
        if offset != (0, 0):
            keys = found.setdefault(offset, [])
            if (b, box) not in keys:
                keys.append((b, box))
    return found


def split(value):
    high = value.astype(BF16)
    return high, (value - high.astype(F32)).astype(BF16)


def dot3(left, right, dims):
    lh, ll = left
    rh, rl = right
    dot = functools.partial(
        lax.dot_general, dimension_numbers=dims, preferred_element_type=F32
    )
    return dot(lh, rh) + (dot(lh, rl) + dot(ll, rh))


def shape(*dims):
    return jax.ShapeDtypeStruct(dims, F32)


def call(kernel, outs, args, flops, scratch=(), in_specs=None, **extra):
    vmem = pl.BlockSpec(memory_space=pltpu.VMEM)
    traffic = sum(4 * a.size for a in list(args) + list(outs))
    return pl.pallas_call(
        kernel,
        out_shape=outs,
        in_specs=in_specs or [vmem] * len(args),
        out_specs=[vmem] * len(outs),
        scratch_shapes=list(scratch),
        compiler_params=pltpu.CompilerParams(vmem_limit_bytes=VMEM_LIMIT),
        cost_estimate=pl.CostEstimate(flops=flops, bytes_accessed=traffic, transcendentals=0),
        **extra,
    )(*args)


SMEM = pl.BlockSpec(memory_space=pltpu.SMEM)
VMEM = pl.BlockSpec(memory_space=pltpu.VMEM)


def prep_kernel(colour, red_ref, near_ref, interp_ref, *outs):
    row, col = BOXES[colour]
    y_refs, r_ref, m_ref = outs[:4], outs[4], outs[5]
    red = red_ref[colour]
    rows = lax.broadcasted_iota(jnp.int32, (SLOTS, SLOTS), 0)
    cols = lax.broadcasted_iota(jnp.int32, (SLOTS, SLOTS), 1)
    masked = jnp.where((rows < red) & (cols + LOW >= red), interp_ref[0, 0], 0.0)
    rows = lax.broadcasted_iota(jnp.int32, (SLOTS, PTS), 0)
    cols = lax.broadcasted_iota(jnp.int32, (SLOTS, PTS), 1)
    wide = jnp.concatenate([jnp.zeros((SLOTS, LOW), F32), masked], axis=1)
    wide = jnp.where((rows == cols) & (rows < red), 1.0, 0.0) - wide
    r_ref[...] = wide
    compress = split(wide)
    for place, offset in enumerate(offsets_of(colour)):
        source = sources_of(colour)[place]
        for at, m in enumerate(children_of(source)):
            target = (BOXES[m][0] - 2 * offset[0], BOXES[m][1] - 2 * offset[1])
            step_row, step_col = target[0] - row, target[1] - col
            block = split(near_ref[0, 0, step_row + 1, step_col + 1])
            value = dot3(compress, block, NN)
            y_refs[place][at] = value
            if (step_row, step_col) == (0, 0):
                centre = split(value)
                m_ref[...] = 0.5 * (
                    dot3(centre, compress, NT) + dot3(compress, centre, NT)
                )


def prep(colour, red, near, interp):
    row, col = BOXES[colour]
    outs = [shape(n, SLOTS, PTS) for n in (4, 2, 2, 1)]
    outs += [shape(SLOTS, PTS), shape(SLOTS, SLOTS)]
    whole = [pl.BlockSpec(o.shape, lambda i, n=len(o.shape): (0,) * n) for o in outs]
    return pl.pallas_call(
        functools.partial(prep_kernel, colour),
        grid=(1,),
        out_shape=outs,
        in_specs=[
            SMEM,
            pl.BlockSpec((1, 1, 3, 3, PTS, PTS), lambda i: (row, col, 0, 0, 0, 0)),
            pl.BlockSpec((1, 1, SLOTS, SLOTS), lambda i: (row, col, 0, 0)),
        ],
        out_specs=whole,
        compiler_params=pltpu.CompilerParams(vmem_limit_bytes=VMEM_LIMIT),
        cost_estimate=pl.CostEstimate(
            flops=9 * 6 * SLOTS * PTS * PTS, bytes_accessed=4 * 2**20, transcendentals=0
        ),
    )(red, near, interp)


def factor_kernel(colour, red_ref, m_ref, out_ref, left_ref, right_ref):
    red = red_ref[colour]
    rows = lax.broadcasted_iota(jnp.int32, (SLOTS, SLOTS), 0)
    cols = lax.broadcasted_iota(jnp.int32, (SLOTS, SLOTS), 1)
    eye = jnp.where(rows == cols, 1.0, 0.0)
    start = jnp.where((rows < red) & (cols < red), m_ref[...], eye)
    left_ref[...] = start[:, :128]
    right_ref[:, : SLOTS - 128] = start[:, 128:]
    right_ref[:, SLOTS - 128 :] = jnp.zeros((SLOTS, 256 - SLOTS), F32)
    sub = lax.broadcasted_iota(jnp.int32, (8, 128), 0)
    lane = lax.broadcasted_iota(jnp.int32, (8, 128), 1)
    full = (8, 128)
    tiles = (left_ref, right_ref)
    for group in range(GROUPS):
        at = slice(8 * group, 8 * group + 8)
        tile, first = (0, 8 * group) if group < 16 else (1, 8 * group - 128)
        held = [ref[at, :] for ref in tiles]
        x = [
            jnp.broadcast_to(held[tile][:, first + s : first + s + 1], full) for s in range(8)
        ]
        low = [jnp.zeros(full, F32) for _ in range(8)]
        for j in range(8):
            here = sub == j
            pivot = jnp.broadcast_to(x[j][j : j + 1, :], full)
            inverse = 1.0 / pivot
            root = lax.rsqrt(pivot)
            scaled = x[j] * inverse
            new = []
            for s in range(8):
                if s == j:
                    new.append(jnp.where(here, inverse, -scaled))
                    low[s] = jnp.where(here, root, low[s])
                else:
                    line = jnp.broadcast_to(x[s][j : j + 1, :], full)
                    new.append(jnp.where(here, line * inverse, x[s] - scaled * line))
                    if s < j:
                        low[s] = jnp.where(here, line * root, low[s])
            x = new
        block = (lane >= first) & (lane < first + 8)
        held[tile] = jnp.where(block, jnp.where(lane - first == sub, 1.0, 0.0), held[tile])
        solved, factor = [], []
        for value in held:
            lines = [jnp.broadcast_to(value[s : s + 1, :], full) for s in range(8)]
            solved.append(sum(x[s] * lines[s] for s in range(8)))
            factor.append(sum(low[s] * lines[s] for s in range(8)))
        factor[tile] = jnp.where(lane < first + 8, factor[tile], 0.0)
        out_ref[at, :128] = factor[0]
        out_ref[at, 128:] = (factor[1] if tile else jnp.zeros(full, F32))[:, : SLOTS - 128]
        lines = [
            [jnp.broadcast_to(value[s : s + 1, :], full) for s in range(8)] for value in solved
        ]
        for later in range(group + 1, GROUPS):
            place = slice(8 * later, 8 * later + 8)
            now = [ref[place, :] for ref in tiles]
            column = [
                jnp.broadcast_to(now[tile][:, first + s : first + s + 1], full)
                for s in range(8)
            ]
            now[tile] = jnp.where(block, 0.0, now[tile])
            for number, ref in enumerate(tiles):
                ref[place, :] = now[number] - sum(
                    column[s] * lines[number][s] for s in range(8)
                )


def factor(colour, red, m):
    scratch = [pltpu.VMEM((SLOTS, 128), F32), pltpu.VMEM((SLOTS, 128), F32)]
    return call(
        functools.partial(factor_kernel, colour),
        [shape(SLOTS, SLOTS)],
        [red, m],
        flops=8 * 10**9,
        scratch=scratch,
        in_specs=[SMEM, VMEM],
    )[0]


def panel_kernel(colour, groups, red_ref, *refs):
    later = later_boxes(colour)
    inverse_refs, z_refs = refs[:4], refs[4:8]
    refs = refs[8:]
    r_refs, m_refs = refs[: len(later)], refs[len(later) : 2 * len(later)]
    refs = refs[2 * len(later) :]
    v_ref, refs = refs[0], refs[1:]
    red = red_ref[colour]
    cols = lax.broadcasted_iota(jnp.int32, (SLOTS, PTS), 1)
    v_ref[...] = jnp.zeros(v_ref.shape, F32)
    if later:
        w_ref, ut_ref = refs[0], refs[1]
        m_outs, send_refs = refs[2 : 2 + len(later)], refs[2 + len(later) :]
    number = 0
    keys = local_keys(colour)
    parts = {}
    for place, source in enumerate(sources_of(colour)):
        inverse = split(inverse_refs[place][...])
        for at, m in enumerate(children_of(source)):
            value = dot3(inverse, split(z_refs[place][at]), NN)
            if source == BOXES[m]:
                value = jnp.where(cols >= red, value, 0.0)
            v_ref[place * SLOTS : (place + 1) * SLOTS, m * SLOTS : (m + 1) * SLOTS] = value[
                :, LOW:
            ]
            if later:
                w_ref[number] = value
                number += 1
            if m > colour:
                parts[(source, BOXES[m])] = split(value)
    for n, r_ref, m_ref, m_out in zip(later, r_refs, m_refs, m_outs if later else ()):
        compress = split(r_ref[...])
        total = m_ref[...]
        for source in sources_of(colour):
            key = (source, BOXES[n])
            if key not in keys:
                continue
            value = dot3(compress, parts[key], NT)
            ut_ref[keys.index(key)] = value
            for ref, group in zip(send_refs, groups):
                if key in group:
                    ref[group.index(key)] = value
            pieces = split(value)
            total = total - dot3(pieces, pieces, NT)
        m_out[...] = total


def panels(colour, red, inverses, z, compressors, ms):
    later = later_boxes(colour)
    wanted = remote_keys(colour)
    offsets = list(wanted)
    groups = [[(moved(b, o), moved(n, o)) for b, n in wanted[o]] for o in offsets]
    outs = [shape(4 * SLOTS, 4 * SLOTS)]
    if later:
        outs += [shape(9, SLOTS, PTS), shape(len(local_keys(colour)), SLOTS, SLOTS)]
        outs += [shape(SLOTS, SLOTS)] * len(later)
        outs += [shape(len(g), SLOTS, SLOTS) for g in groups]
    args = [red, *inverses, *z, *[compressors[n] for n in later], *[ms[n] for n in later]]
    got = call(
        functools.partial(panel_kernel, colour, groups),
        outs,
        args,
        flops=9 * 6 * SLOTS * SLOTS * PTS,
        in_specs=[SMEM] + [VMEM] * (len(args) - 1),
    )
    if not later:
        return got[0]
    ms = dict(zip(later, got[3 : 3 + len(later)]))
    sends = dict(zip(offsets, got[3 + len(later) :]))
    return got[0], got[1], got[2], ms, sends


def update_kernel(colour, offsets, *refs):
    later = later_boxes(colour)
    w_ref, ut_ref = refs[0], refs[1]
    received = dict(zip(offsets, refs[2 : 2 + len(offsets)]))
    refs = refs[2 + len(offsets) :]
    count = 4 * len(later)
    ins, outs = refs[:count], refs[count : 2 * count]
    wh_ref, wl_ref = refs[2 * count :]
    pairs = pairs_of(colour)
    wanted = remote_keys(colour)
    own = local_keys(colour)
    for i in range(9):
        wh_ref[i], wl_ref[i] = split(w_ref[i])
    terms = update_terms(colour)
    for number, c in enumerate(later):
        for place, box in enumerate(sources_of(c)):
            offset = offsets_of(c)[place]
            pieces = {}
            for at, m in enumerate(children_of(box)):
                total = ins[4 * number + place][at]
                for t in terms:
                    if t[:3] != (c, place, m):
                        continue
                    key = t[3:]
                    if key not in pieces:
                        if offset == (0, 0):
                            value = ut_ref[own.index(key)]
                        else:
                            value = received[offset][wanted[offset].index(key)]
                        pieces[key] = split(value)
                    i = pairs.index((t[3], m))
                    total = total - dot3(pieces[key], (wh_ref[i], wl_ref[i]), NN)
                outs[4 * number + place][at] = total


def update(colour, w, ut, received, z):
    later = later_boxes(colour)
    offsets = list(received)
    flat = [array for c in later for array in z[c]]
    args = [w, ut, *[received[o] for o in offsets], *flat]
    first = 2 + len(offsets)
    got = call(
        functools.partial(update_kernel, colour, offsets),
        [shape(*a.shape) for a in flat],
        args,
        flops=len(update_terms(colour)) * 6 * SLOTS * SLOTS * PTS,
        scratch=[pltpu.VMEM((9, SLOTS, PTS), BF16)] * 2,
        input_output_aliases={first + i: i for i in range(len(flat))},
    )
    return {c: list(got[4 * i : 4 * i + 4]) for i, c in enumerate(later)}


def base_kernel(near_ref, out_ref):
    x = pl.program_id(0)
    for number, (row, col) in enumerate(BOXES):

        @pl.when(x == number)
        def _():
            for y, (other_row, other_col) in enumerate(BOXES):
                block = near_ref[0, 0, other_row - row + 1, other_col - col + 1]
                out_ref[:, y * SLOTS : (y + 1) * SLOTS] = block[LOW:, LOW:]


def base(near):
    return pl.pallas_call(
        base_kernel,
        grid=(4,),
        out_shape=shape(4 * SLOTS, 4 * SLOTS),
        in_specs=[
            pl.BlockSpec((1, 1, 3, 3, PTS, PTS), lambda i: (i // 2, i % 2, 0, 0, 0, 0)),
        ],
        out_specs=pl.BlockSpec((SLOTS, 4 * SLOTS), lambda i: (i, 0)),
        compiler_params=pltpu.CompilerParams(vmem_limit_bytes=VMEM_LIMIT),
        cost_estimate=pl.CostEstimate(
            flops=0, bytes_accessed=12 * 2**20, transcendentals=0
        ),
    )(near)


def gather_kernel(last, red_ref, total_ref, v_ref, out_ref):
    high, low = split(v_ref[...])
    for i in range(5):
        rows = slice(128 * i, 128 * i + 128)
        value = total_ref[rows, :] - dot3((high[:, rows], low[:, rows]), (high, low), TN)
        if last:
            dims = (128, 4 * SLOTS)
            marks = []
            for axis, start in ((0, 128 * i), (1, 0)):
                place = lax.broadcasted_iota(jnp.int32, dims, axis) + start
                mark = jnp.zeros(dims, jnp.int32)
                for n in range(4):
                    inside = (place >= n * SLOTS) & (place < (n + 1) * SLOTS)
                    kept = inside & (place - n * SLOTS + LOW >= red_ref[n])
                    mark = jnp.where(kept, 1, mark)
                marks.append(mark)
            value = jnp.where((marks[0] * marks[1]) > 0, value, 0.0)
        out_ref[rows, :] = value


def gather(last, red, total, v):
    return call(
        functools.partial(gather_kernel, last),
        [shape(4 * SLOTS, 4 * SLOTS)],
        [red, total, v],
        flops=6 * (4 * SLOTS) ** 3,
        in_specs=[SMEM, VMEM, VMEM],
        input_output_aliases={1: 0},
    )[0]


def fetch(value, offset):
    rows, cols = lax.axis_size("row"), lax.axis_size("col")
    pairs = []
    for i in range(rows):
        for j in range(cols):
            a, b = i + offset[0], j + offset[1]
            if 0 <= a < rows and 0 <= b < cols:
                pairs.append((a * cols + b, i * cols + j))
    return lax.ppermute(value, ("row", "col"), pairs)


def from_partner(value, axis):
    pairs = [(source, source ^ 1) for source in range(lax.axis_size(axis))]
    return lax.ppermute(value, axis, pairs)


def local(near, interp, red_count, owner_flip):
    red = red_count.reshape(4)
    z, compressors, ms = {}, {}, {}
    inverse = None
    for c in range(4):
        *y, compressors[c], ms[c] = prep(c, red, near, interp)
        z[c] = [y[0]] + [fetch(y[p], offsets_of(c)[p]) for p in (1, 2, 3)]
    total = base(near)
    for c in range(4):
        inverse = factor(c, red, ms[c])
        inverses = [inverse] + [fetch(inverse, o) for o in offsets_of(c)[1:]]
        if c < 3:
            v, w, ut, new, sends = panels(c, red, inverses, z[c], compressors, ms)
            ms.update(new)
            received = {o: fetch(s, o) for o, s in sends.items()}
            z.update(update(c, w, ut, received, z))
        else:
            v = panels(c, red, inverses, z[c], compressors, ms)
        total = gather(c == 3, red, total, v)
    flip = owner_flip[0, 0]
    total = jnp.where(flip[0] == 1, from_partner(total, "row"), total)
    total = jnp.where(flip[1] == 1, from_partner(total, "col"), total)
    return total[None, None]


def solution(mesh):
    in_specs = (
        P("row", "col", None, None, None, None),
        P("row", "col", None, None),
        P("row", "col"),
        P("row", "col", None),
    )
    out_specs = P("row", "col", None, None)
    return jax.shard_map(local, mesh=mesh, in_specs=in_specs, out_specs=out_specs, check_vma=False)
```

```python
import functools

import jax
import jax.numpy as jnp
from jax import lax
from jax.experimental import pallas as pl
from jax.experimental.pallas import tpu as pltpu
from jax.sharding import PartitionSpec as P

BOXES = ((0, 0), (0, 1), (1, 0), (1, 1))
PTS = 256
SLOTS = 160
LOW = 96
GROUPS = SLOTS // 8
VMEM_LIMIT = 48 * 2**20
F32 = jnp.float32
BF16 = jnp.bfloat16
NN = (((1,), (0,)), ((), ()))
NT = (((1,), (1,)), ((), ()))
TN = (((0,), (0,)), ((), ()))


def near_each_other(a, b):
    return abs(a[0] - b[0]) <= 1 and abs(a[1] - b[1]) <= 1


def offsets_of(colour):
    row, col = BOXES[colour]
    step_row, step_col = 1 - 2 * row, 1 - 2 * col
    return ((0, 0), (0, step_col), (step_row, 0), (step_row, step_col))


def sources_of(colour):
    row, col = BOXES[colour]
    return [(row + 2 * dr, col + 2 * dc) for dr, dc in offsets_of(colour)]


def children_of(box):
    return [m for m in range(4) if near_each_other(BOXES[m], box)]


def moved(box, offset):
    return (box[0] - 2 * offset[0], box[1] - 2 * offset[1])


def pairs_of(colour):
    return [(b, m) for b in sources_of(colour) for m in children_of(b)]


def later_boxes(colour):
    return list(range(colour + 1, 4))


def local_keys(colour):
    return [
        (b, BOXES[n]) for n in later_boxes(colour) for b in sources_of(colour)
        if near_each_other(b, BOXES[n])
    ]


def update_terms(later, colour):
    terms = []
    for place, box in enumerate(sources_of(later)):
        for m in children_of(box):
            for b in sources_of(colour):
                if near_each_other(b, box) and near_each_other(b, BOXES[m]):
                    terms.append((place, m, b, box))
    return terms


def message_keys(later, place, colours):
    found = []
    for colour in colours:
        for at, _, b, box in update_terms(later, colour):
            if at == place and (b, box) not in found:
                found.append((b, box))
    return found


def sent_keys(later, place, colours):
    offset = offsets_of(later)[place]
    return [(moved(b, offset), moved(n, offset)) for b, n in message_keys(later, place, colours)]


PIECE = SLOTS * SLOTS // 128
PANEL = SLOTS * PTS // 128
TAIL = PIECE - SLOTS


def pack(value):
    rest = value[:, 128:]
    return value[:, :128], jnp.concatenate(
        [rest[TAIL * i : TAIL * (i + 1)] for i in range(4)], axis=1
    )


def store_piece(ref, row, value):
    head, tail = pack(value)
    ref[row : row + SLOTS, :] = head
    ref[row + SLOTS : row + PIECE, :] = tail


def store_panel(ref, row, value, rows):
    if rows == PIECE:
        store_piece(ref, row, value[:, LOW:])
    else:
        ref[row : row + SLOTS, :] = value[:, :128]
        ref[row + SLOTS : row + PANEL, :] = value[:, 128:]


def load_panel(ref, row, rows):
    if rows == PIECE:
        return jnp.concatenate([jnp.zeros((SLOTS, LOW), F32), load_piece(ref, row)], axis=1)
    return jnp.concatenate(
        [ref[row : row + SLOTS, :], ref[row + SLOTS : row + PANEL, :]], axis=1
    )


def panel_rows(colour, m):
    return PIECE if m < colour else PANEL


def layout(colour, colours):
    panels, pieces = {}, {}
    row = 0
    for place in (1, 3):
        for m in children_of(sources_of(colour)[place]):
            panels[place, m] = (0, row)
            row += panel_rows(colour, m)
    for key in message_keys(colour, 1, colours):
        pieces[1, key] = (0, row)
        row += PIECE
    sizes = [row]
    row = 0
    for place in (2, 3):
        for m in children_of(sources_of(colour)[place]):
            if place == 2:
                panels[place, m] = (1, row)
                row += panel_rows(colour, m)
        if place == 3:
            break
        for key in message_keys(colour, 2, colours):
            pieces[2, key] = (1, row)
            row += PIECE
    own = row
    (m,) = children_of(sources_of(colour)[3])
    forwarded = [(panels[3, m][1], panel_rows(colour, m))]
    panels[3, m] = (1, row)
    row += panel_rows(colour, m)
    offset = offsets_of(colour)[2]
    for key in message_keys(colour, 3, colours):
        here = (moved(key[0], offset), moved(key[1], offset))
        forwarded.append((pieces[1, here][1], PIECE))
        pieces[3, key] = (1, row)
        row += PIECE
    sizes.append(row)
    return panels, pieces, sizes, own, forwarded


def load_piece(ref, row):
    tail = ref[row + SLOTS : row + PIECE, :]
    width = SLOTS - 128
    rest = jnp.concatenate([tail[:, width * i : width * (i + 1)] for i in range(4)], axis=0)
    return jnp.concatenate([ref[row : row + SLOTS, :], rest], axis=1)


def split(value):
    high = value.astype(BF16)
    return high, (value - high.astype(F32)).astype(BF16)


def dot3(left, right, dims):
    lh, ll = left
    rh, rl = right
    dot = functools.partial(
        lax.dot_general, dimension_numbers=dims, preferred_element_type=F32
    )
    return dot(lh, rh) + (dot(lh, rl) + dot(ll, rh))


def shape(*dims):
    return jax.ShapeDtypeStruct(dims, F32)


def call(kernel, outs, args, flops, scratch=(), in_specs=None, **extra):
    vmem = pl.BlockSpec(memory_space=pltpu.VMEM)
    traffic = sum(4 * a.size for a in list(args) + list(outs))
    return pl.pallas_call(
        kernel,
        out_shape=outs,
        in_specs=in_specs or [vmem] * len(args),
        out_specs=[vmem] * len(outs),
        scratch_shapes=list(scratch),
        compiler_params=pltpu.CompilerParams(vmem_limit_bytes=VMEM_LIMIT),
        cost_estimate=pl.CostEstimate(flops=flops, bytes_accessed=traffic, transcendentals=0),
        **extra,
    )(*args)


SMEM = pl.BlockSpec(memory_space=pltpu.SMEM)
VMEM = pl.BlockSpec(memory_space=pltpu.VMEM)


def prep_kernel(colour, red_ref, near_ref, interp_ref, *outs):
    row, col = BOXES[colour]
    own_ref, col_ref, row_ref, r_ref, m_ref, base_ref = outs
    lines = {1: [col_ref, 0], 2: [row_ref, 0]}
    red = red_ref[colour]
    rows = lax.broadcasted_iota(jnp.int32, (SLOTS, SLOTS), 0)
    cols = lax.broadcasted_iota(jnp.int32, (SLOTS, SLOTS), 1)
    for number, (other_row, other_col) in enumerate(BOXES):
        block = near_ref[0, 0, other_row - row + 1, other_col - col + 1]
        kept = (rows + LOW >= red) & (cols + LOW >= red_ref[number])
        base_ref[:, number * SLOTS : (number + 1) * SLOTS] = jnp.where(
            kept, block[LOW:, LOW:], 0.0
        )
    masked = jnp.where((rows < red) & (cols + LOW >= red), interp_ref[0, 0], 0.0)
    rows = lax.broadcasted_iota(jnp.int32, (SLOTS, PTS), 0)
    cols = lax.broadcasted_iota(jnp.int32, (SLOTS, PTS), 1)
    wide = jnp.concatenate([jnp.zeros((SLOTS, LOW), F32), masked], axis=1)
    wide = jnp.where((rows == cols) & (rows < red), 1.0, 0.0) - wide
    r_ref[...] = wide
    compress = split(wide)
    for place in (0, 1, 3, 2):
        offset, source = offsets_of(colour)[place], sources_of(colour)[place]
        for at, m in enumerate(children_of(source)):
            target = (BOXES[m][0] - 2 * offset[0], BOXES[m][1] - 2 * offset[1])
            step_row, step_col = target[0] - row, target[1] - col
            block = split(near_ref[0, 0, step_row + 1, step_col + 1])
            value = dot3(compress, block, NN)
            if place:
                line = lines[2 if place == 2 else 1]
                store_panel(line[0], line[1], value, panel_rows(colour, m))
                line[1] += panel_rows(colour, m)
            else:
                own_ref[at] = value
            if (step_row, step_col) == (0, 0):
                centre = split(value)
                m_ref[...] = 0.5 * (
                    dot3(centre, compress, NT) + dot3(compress, centre, NT)
                )


def prep(colour, red, near, interp):
    row, col = BOXES[colour]
    _, _, sizes, own, _ = layout(colour, ())
    outs = [shape(4, SLOTS, PTS), shape(sizes[0], 128), shape(own, 128)]
    outs += [shape(SLOTS, PTS), shape(SLOTS, SLOTS), shape(SLOTS, 4 * SLOTS)]
    whole = [pl.BlockSpec(o.shape, lambda i, n=len(o.shape): (0,) * n) for o in outs]
    return pl.pallas_call(
        functools.partial(prep_kernel, colour),
        grid=(1,),
        out_shape=outs,
        in_specs=[
            SMEM,
            pl.BlockSpec((1, 1, 3, 3, PTS, PTS), lambda i: (row, col, 0, 0, 0, 0)),
            pl.BlockSpec((1, 1, SLOTS, SLOTS), lambda i: (row, col, 0, 0)),
        ],
        out_specs=whole,
        compiler_params=pltpu.CompilerParams(vmem_limit_bytes=VMEM_LIMIT),
        cost_estimate=pl.CostEstimate(
            flops=9 * 6 * SLOTS * PTS * PTS, bytes_accessed=4 * 2**20, transcendentals=0
        ),
    )(red, near, interp)


def eliminate(start, out_ref, left_ref, right_ref):
    left_ref[...] = start[:, :128]
    right_ref[:, : SLOTS - 128] = start[:, 128:]
    right_ref[:, SLOTS - 128 :] = jnp.zeros((SLOTS, 256 - SLOTS), F32)
    sub = lax.broadcasted_iota(jnp.int32, (8, 128), 0)
    lane = lax.broadcasted_iota(jnp.int32, (8, 128), 1)
    full = (8, 128)
    tiles = (left_ref, right_ref)
    for group in range(GROUPS):
        at = slice(8 * group, 8 * group + 8)
        tile, first = (0, 8 * group) if group < 16 else (1, 8 * group - 128)
        held = [ref[at, :] for ref in tiles]
        x = [
            jnp.broadcast_to(held[tile][:, first + s : first + s + 1], full) for s in range(8)
        ]
        low = [jnp.zeros(full, F32) for _ in range(8)]
        for j in range(8):
            here = sub == j
            pivot = jnp.broadcast_to(x[j][j : j + 1, :], full)
            inverse = 1.0 / pivot
            root = lax.rsqrt(pivot)
            scaled = x[j] * inverse
            new = []
            for s in range(8):
                if s == j:
                    new.append(jnp.where(here, inverse, -scaled))
                    low[s] = jnp.where(here, root, low[s])
                else:
                    line = jnp.broadcast_to(x[s][j : j + 1, :], full)
                    new.append(jnp.where(here, line * inverse, x[s] - scaled * line))
                    if s < j:
                        low[s] = jnp.where(here, line * root, low[s])
            x = new
        block = (lane >= first) & (lane < first + 8)
        held[tile] = jnp.where(block, jnp.where(lane - first == sub, 1.0, 0.0), held[tile])
        solved, factor = [], []
        for value in held:
            lines = [jnp.broadcast_to(value[s : s + 1, :], full) for s in range(8)]
            solved.append(sum(x[s] * lines[s] for s in range(8)))
            factor.append(sum(low[s] * lines[s] for s in range(8)))
        factor[tile] = jnp.where(lane < first + 8, factor[tile], 0.0)
        out_ref[at, :128] = factor[0]
        out_ref[at, 128:] = (factor[1] if tile else jnp.zeros(full, F32))[:, : SLOTS - 128]
        lines = [
            [jnp.broadcast_to(value[s : s + 1, :], full) for s in range(8)] for value in solved
        ]
        for later in range(group + 1, GROUPS):
            place = slice(8 * later, 8 * later + 8)
            now = [ref[place, :] for ref in tiles]
            column = [
                jnp.broadcast_to(now[tile][:, first + s : first + s + 1], full)
                for s in range(8)
            ]
            now[tile] = jnp.where(block, 0.0, now[tile])
            for number, ref in enumerate(tiles):
                ref[place, :] = now[number] - sum(
                    column[s] * lines[number][s] for s in range(8)
                )


def factor_kernel(colour, keys, red_ref, m_ref, *refs):
    ut_ref = refs[0] if colour else None
    out_ref, *message_refs, left_ref, right_ref = refs[1:] if colour else refs
    red = red_ref[colour]
    rows = lax.broadcasted_iota(jnp.int32, (SLOTS, SLOTS), 0)
    cols = lax.broadcasted_iota(jnp.int32, (SLOTS, SLOTS), 1)
    eye = jnp.where(rows == cols, 1.0, 0.0)
    start = jnp.where((rows < red) & (cols < red), m_ref[...], eye)
    for place, ref in enumerate(message_refs, 1):
        for i, key in enumerate(sent_keys(colour, place, [colour - 1]) if colour else ()):
            store_piece(ref, PIECE * (i + 1), ut_ref[keys.index(key)])
    eliminate(start, out_ref, left_ref, right_ref)
    head, tail = pack(out_ref[...])
    for ref in message_refs:
        ref[:SLOTS, :] = head
        ref[SLOTS:PIECE, :] = tail


def factor(colour, red, m, ut):
    scratch = [pltpu.VMEM((SLOTS, 128), F32), pltpu.VMEM((SLOTS, 128), F32)]
    before = [colour - 1] if colour else []
    sizes = [1 + len(sent_keys(colour, place, before)) for place in (1, 2, 3)]
    args = [red, m] + ([ut] if colour else [])
    return call(
        functools.partial(factor_kernel, colour, local_keys(colour - 1) if colour else ()),
        [shape(SLOTS, SLOTS)] + [shape(n * PIECE, 128) for n in sizes],
        args,
        flops=8 * 10**9,
        scratch=scratch,
        in_specs=[SMEM] + [VMEM] * (len(args) - 1),
    )


class Pieces:
    def __init__(self, make):
        self.make, self.held = make, {}

    def __getitem__(self, key):
        if key not in self.held:
            self.held[key] = split(self.make(key))
        return self.held[key]


def early_kernel(later, *refs):
    colours = range(later - 1)
    own_ref, *message_refs = refs[:3]
    refs = refs[3:]
    panels, spots, *_ = layout(later, colours)
    ut_refs, w_refs = refs[: later - 1], refs[later - 1 : 2 * (later - 1)]
    outs = refs[2 * (later - 1) :]
    panel_of = {}
    for c in colours:
        for i, (b, m) in enumerate(pairs_of(c)):
            panel_of[b, m] = (c, i)
    colour_of = {b: c for c in colours for b in sources_of(c)}
    w = Pieces(lambda key: w_refs[panel_of[key][0]][panel_of[key][1]])
    for place, box in enumerate(sources_of(later)):
        children = children_of(box)
        if place:
            u = Pieces(
                lambda key: load_piece(message_refs[spots[place, key][0]], spots[place, key][1])
            )
        else:
            u = Pieces(
                lambda key: ut_refs[colour_of[key[0]]][local_keys(colour_of[key[0]]).index(key)]
            )
        for at, m in enumerate(children):
            if place:
                side, row = panels[place, m]
                total = load_panel(message_refs[side], row, panel_rows(later, m))
            else:
                total = own_ref[at]
            for c in colours:
                for t in update_terms(later, c):
                    if t[:2] == (place, m):
                        total = total - dot3(u[t[2:]], w[t[2], m], NN)
            outs[place][at] = total


def early(later, own, messages, uts, ws):
    colours = range(later - 1)
    args = [own, *messages, *[uts[c] for c in colours], *[ws[c] for c in colours]]
    terms = sum(len(update_terms(later, c)) for c in colours)
    return call(
        functools.partial(early_kernel, later),
        [shape(n, SLOTS, PTS) for n in (4, 2, 2, 1)],
        args,
        flops=terms * 6 * SLOTS * SLOTS * PTS,
    )


def stage_kernel(colour, red_ref, *refs):
    later = later_boxes(colour)
    far = colour + 2
    refs = list(refs)

    def take(count):
        taken, refs[:] = refs[:count], refs[count:]
        return taken

    (inverse_ref,) = take(1)
    message_refs = take(3)
    z_refs = take(4 if colour > 1 else 3)
    panels = layout(colour, ())[0]
    if colour:
        before_w, before_ut = take(2)
    r_refs, m_refs = take(len(later)), take(len(later))
    y_refs = take(2) if far < 4 else []
    old_refs = take(colour) if far < 4 else []
    (v_ref,) = take(1)
    if later:
        w_ref, ut_ref = take(2)
    m_outs = take(len(later))
    send_refs = take(2) if far < 4 else []

    red = red_ref[colour]
    cols = lax.broadcasted_iota(jnp.int32, (SLOTS, PTS), 1)
    slots = lax.broadcasted_iota(jnp.int32, (SLOTS, SLOTS), 1)
    v_ref[...] = jnp.zeros(v_ref.shape, F32)
    keys = local_keys(colour)
    parts = {}
    if colour:
        before = pairs_of(colour - 1)
        own_keys = local_keys(colour - 1)
        old_w = Pieces(lambda key: before_w[before.index(key)])
    number = 0
    for place, source in enumerate(sources_of(colour)):
        if place:
            ref = message_refs[place - 1]
            inverse = split(load_piece(ref, 0))
            names = message_keys(colour, place, [colour - 1]) if colour else []
            u = Pieces(lambda key: load_piece(ref, PIECE * (names.index(key) + 1)))
        else:
            inverse = split(inverse_ref[...])
            u = Pieces(lambda key: before_ut[own_keys.index(key)])
        for at, m in enumerate(children_of(source)):
            if colour > 1 or not place:
                value = z_refs[place][at]
            else:
                side, row = panels[place, m]
                value = load_panel(z_refs[1 + side], row, panel_rows(colour, m))
            for t in update_terms(colour, colour - 1) if colour else ():
                if t[:2] == (place, m):
                    value = value - dot3(u[t[2:]], old_w[t[2], m], NN)
            value = dot3(inverse, split(value), NN)
            if source == BOXES[m]:
                value = jnp.where(cols >= red, value, 0.0)
            v_ref[place * SLOTS : (place + 1) * SLOTS, m * SLOTS : (m + 1) * SLOTS] = jnp.where(
                slots + LOW >= red_ref[m], value[:, LOW:], 0.0
            )
            if later:
                w_ref[number] = value
                number += 1
            if m > colour:
                parts[(source, BOXES[m])] = split(value)
    made = {}
    for n, r_ref, m_ref, m_out in zip(later, r_refs, m_refs, m_outs):
        compress = split(r_ref[...])
        total = m_ref[...]
        for source in sources_of(colour):
            key = (source, BOXES[n])
            if key not in keys:
                continue
            value = dot3(compress, parts[key], NT)
            ut_ref[keys.index(key)] = value
            made[key] = value
            pieces = split(value)
            total = total - dot3(pieces, pieces, NT)
        m_out[...] = total
    for place, (y_ref, ref) in enumerate(zip(y_refs, send_refs), 1):
        row = y_ref.shape[0]
        ref[:row, :] = y_ref[...]
        for key in sent_keys(far, place, range(far - 1)):
            if key in made:
                value = made[key]
            else:
                (c,) = [c for c in range(colour) if key in local_keys(c)]
                value = old_refs[c][local_keys(c).index(key)]
            store_piece(ref, row, value)
            row += PIECE


def stage(colour, red, inverse, messages, z, before, compressors, ms, y, uts):
    later = later_boxes(colour)
    far = colour + 2
    args = [red, inverse, *messages, *z, *before]
    args += [compressors[n] for n in later] + [ms[n] for n in later]
    outs = [shape(4 * SLOTS, 4 * SLOTS)]
    if later:
        outs += [shape(9, SLOTS, PTS), shape(len(local_keys(colour)), SLOTS, SLOTS)]
        outs += [shape(SLOTS, SLOTS)] * len(later)
    if far < 4:
        args += y[far][1:] + [uts[c] for c in range(colour)]
        _, _, sizes, own, _ = layout(far, range(far - 1))
        outs += [shape(sizes[0], 128), shape(own, 128)]
    got = call(
        functools.partial(stage_kernel, colour),
        outs,
        args,
        flops=25 * 6 * SLOTS * SLOTS * PTS,
        in_specs=[SMEM] + [VMEM] * (len(args) - 1),
    )
    v, got = got[0], got[1:]
    if not later:
        return v, None, None, {}, []
    w, ut, got = got[0], got[1], got[2:]
    return v, w, ut, dict(zip(later, got)), got[len(later) :]


TILES = 4 * SLOTS // 128
TRIANGLE = [(i, j) for i in range(TILES) for j in range(i, TILES)]


def gather_kernel(first, v_ref, *refs):
    out_ref = refs[-1]
    high, low = split(v_ref[...])
    for i in range(TILES):
        rows = slice(128 * i, 128 * i + 128)
        value = dot3(
            (high[:, rows], low[:, rows]), (high[:, 128 * i :], low[:, 128 * i :]), TN
        )
        for j in range(i, TILES):
            at = 128 * TRIANGLE.index((i, j))
            block = value[:, 128 * (j - i) : 128 * (j - i) + 128]
            if not first:
                block = block + refs[0][at : at + 128, :]
            out_ref[at : at + 128, :] = block


def gather(v, total=None):
    first = total is None
    return call(
        functools.partial(gather_kernel, first),
        [shape(128 * len(TRIANGLE), 128)],
        [v] if first else [v, total],
        flops=6 * (4 * SLOTS) ** 3,
        **({} if first else {"input_output_aliases": {1: 0}}),
    )[0]


def finish_kernel(flip_ref, base_ref, other_ref, mine_ref, theirs_ref, out_ref):
    swap = flip_ref[1] == 1
    pick = lambda at: jnp.where(swap, other_ref[at], base_ref[at])
    for number, (i, j) in enumerate(TRIANGLE):
        at = slice(128 * number, 128 * number + 128)
        block = jnp.where(swap, theirs_ref[at, :], mine_ref[at, :])
        rows, cols = slice(128 * i, 128 * i + 128), slice(128 * j, 128 * j + 128)
        out_ref[rows, cols] = pick((rows, cols)) - block
        if i != j:
            out_ref[cols, rows] = pick((cols, rows)) - block.T


def finish(flip, base, other, mine, theirs):
    return call(
        finish_kernel,
        [shape(4 * SLOTS, 4 * SLOTS)],
        [flip, base, other, mine, theirs],
        flops=(4 * SLOTS) ** 2,
        in_specs=[SMEM, VMEM, VMEM, VMEM, VMEM],
    )[0]


def fetch(value, offset):
    rows, cols = lax.axis_size("row"), lax.axis_size("col")
    pairs = []
    for i in range(rows):
        for j in range(cols):
            a, b = i + offset[0], j + offset[1]
            if 0 <= a < rows and 0 <= b < cols:
                pairs.append((a * cols + b, i * cols + j))
    return lax.ppermute(value, ("row", "col"), pairs)


def from_partner(value, axis):
    pairs = [(source, source ^ 1) for source in range(lax.axis_size(axis))]
    return lax.ppermute(value, axis, pairs)


def after(value, *others):
    return lax.optimization_barrier((value, *others))[0]


def local(near, interp, red_count, owner_flip):
    red = red_count.reshape(4)
    y, compressors, ms, uts, ws = {}, {}, {}, {}, {}

    def fetch_all(values, colour):
        return [fetch(value, o) for value, o in zip(values, offsets_of(colour)[1:])]

    def prepare(colour, red):
        *y[colour], compressors[colour], ms[colour], base[colour] = prep(
            colour, red, near, interp
        )

    def forward(colour, colours, got, own):
        pieces = [got[row : row + rows] for row, rows in layout(colour, colours)[4]]
        return jnp.concatenate([own, *pieces], axis=0)

    base = {}
    prepare(0, red)
    arrived = {0: [fetch(y[0][1], offsets_of(0)[1])]}
    prepare(1, red)
    arrived[1] = [fetch(y[1][1], offsets_of(1)[1])]
    flip = owner_flip[0, 0]
    total = None
    for c in range(4):
        tied = red if c else after(red, compressors[1])
        inverse, *messages = factor(c, tied, ms[c], uts.get(c - 1))
        late = fetch_all(messages, c)
        if c == 0:
            got = [after(arrived[n][0], inverse) for n in (0, 1)]
            both = [forward(n, (), got[n], y[n][2]) for n in (0, 1)]
            cut = both[0].shape[0]
            both = fetch(jnp.concatenate(both, axis=0), offsets_of(0)[2])
            arrived[0].append(both[:cut])
            arrived[1].append(both[cut:])
            tied = after(red, inverse)
            prepare(2, tied)
            prepare(3, tied)
        if c > 1:
            z = early(c, y[c][0], arrived[c], uts, ws)
        else:
            z = [y[c][0], *arrived[c]]
        if c:
            total = gather(v, total)
        before = [ws[c - 1], uts[c - 1]] if c else []
        tied = red
        if c == 1:
            tied = after(red, start)
        if c == 3:
            tied = after(red, other)
        v, ws[c], uts[c], new, sends = stage(
            c, tied, inverse, late, z, before, compressors, ms, y, uts
        )
        ms.update(new)
        if sends:
            far, known = c + 2, range(c + 1)
            got = fetch(sends[0], offsets_of(far)[1])
            row = forward(far, known, got, sends[1])
            arrived[far] = [got, fetch(row, offsets_of(far)[2])]
        if c == 0:
            start = jnp.concatenate([base[n] for n in range(4)], axis=0)
            start = after(start, v)
            start = jnp.where(flip[0] == 1, from_partner(start, "row"), start)
        if c == 1:
            other = from_partner(start, "col")
    total = gather(v, total)
    total = jnp.where(flip[0] == 1, from_partner(total, "row"), total)
    return finish(flip, start, other, total, from_partner(total, "col"))[None, None]


def solution(mesh):
    in_specs = (
        P("row", "col", None, None, None, None),
        P("row", "col", None, None),
        P("row", "col"),
        P("row", "col", None),
    )
    out_specs = P("row", "col", None, None)
    return jax.shard_map(local, mesh=mesh, in_specs=in_specs, out_specs=out_specs, check_vma=False)
```

```python
import functools

import jax
import jax.numpy as jnp
from jax import lax
from jax.experimental import pallas as pl
from jax.experimental.pallas import tpu as pltpu
from jax.sharding import PartitionSpec as P

BOXES = ((0, 0), (0, 1), (1, 0), (1, 1))
PTS = 256
SLOTS = 160
LOW = 96
GROUPS = SLOTS // 8
VMEM_LIMIT = 24 * 2**20
PREP_VMEM_LIMIT = 48 * 2**20
F32 = jnp.float32
BF16 = jnp.bfloat16
NN = (((1,), (0,)), ((), ()))
NT = (((1,), (1,)), ((), ()))
TN = (((0,), (0,)), ((), ()))


def near_each_other(a, b):
    return abs(a[0] - b[0]) <= 1 and abs(a[1] - b[1]) <= 1


def offsets_of(colour):
    row, col = BOXES[colour]
    step_row, step_col = 1 - 2 * row, 1 - 2 * col
    return ((0, 0), (0, step_col), (step_row, 0), (step_row, step_col))


def sources_of(colour):
    row, col = BOXES[colour]
    return [(row + 2 * dr, col + 2 * dc) for dr, dc in offsets_of(colour)]


def children_of(box):
    return [m for m in range(4) if near_each_other(BOXES[m], box)]


def moved(box, offset):
    return (box[0] - 2 * offset[0], box[1] - 2 * offset[1])


def pairs_of(colour):
    return [(b, m) for b in sources_of(colour) for m in children_of(b)]


def later_boxes(colour):
    return list(range(colour + 1, 4))


def local_keys(colour):
    return [
        (b, BOXES[n]) for n in later_boxes(colour) for b in sources_of(colour)
        if near_each_other(b, BOXES[n])
    ]


def update_terms(later, colour):
    terms = []
    for place, box in enumerate(sources_of(later)):
        for m in children_of(box):
            for b in sources_of(colour):
                if near_each_other(b, box) and near_each_other(b, BOXES[m]):
                    terms.append((place, m, b, box))
    return terms


def message_keys(later, place, colours):
    found = []
    for colour in colours:
        for at, _, b, box in update_terms(later, colour):
            if at == place and (b, box) not in found:
                found.append((b, box))
    return found


def sent_keys(later, place, colours):
    offset = offsets_of(later)[place]
    return [(moved(b, offset), moved(n, offset)) for b, n in message_keys(later, place, colours)]


PIECE = SLOTS * SLOTS // 128
PANEL = SLOTS * PTS // 128
TAIL = PIECE - SLOTS


def pack(value):
    rest = value[:, 128:]
    return value[:, :128], jnp.concatenate(
        [rest[TAIL * i : TAIL * (i + 1)] for i in range(4)], axis=1
    )


def store_piece(ref, row, value):
    head, tail = pack(value)
    ref[row : row + SLOTS, :] = head
    ref[row + SLOTS : row + PIECE, :] = tail


FACTOR = PIECE - 64


def store_factor(ref, row, value):
    last = value[128:, :128]
    block = jnp.concatenate([last[:, :64], last[:, 64:]], axis=0)
    ref[row : row + 64, :] = jnp.concatenate([value[:64, :64], block], axis=1)
    ref[row + 64 : row + 128, :] = value[64:128, :128]
    rest = value[128:, 128:]
    ref[row + 128 : row + FACTOR, :] = jnp.concatenate(
        [rest[8 * i : 8 * i + 8] for i in range(4)], axis=1
    )


def load_factor(ref, row):
    first = ref[row : row + 64, :]
    block = first[:, 64:]
    last = jnp.concatenate([block[:32], block[32:]], axis=1)
    lane = lax.broadcasted_iota(jnp.int32, first.shape, 1)
    first = jnp.where(lane < 64, first, 0.0)
    left = jnp.concatenate([first, ref[row + 64 : row + 128, :], last], axis=0)
    tail = ref[row + 128 : row + FACTOR, :]
    rest = jnp.concatenate([tail[:, 32 * i : 32 * i + 32] for i in range(4)], axis=0)
    right = jnp.concatenate([jnp.zeros((128, 32), F32), rest], axis=0)
    return jnp.concatenate([left, right], axis=1)


def store_panel(ref, row, value, rows):
    if rows == PIECE:
        store_piece(ref, row, value[:, LOW:])
    else:
        ref[row : row + SLOTS, :] = value[:, :128]
        ref[row + SLOTS : row + PANEL, :] = value[:, 128:]


def load_panel(ref, row, rows):
    if rows == PIECE:
        return jnp.concatenate([jnp.zeros((SLOTS, LOW), F32), load_piece(ref, row)], axis=1)
    return jnp.concatenate(
        [ref[row : row + SLOTS, :], ref[row + SLOTS : row + PANEL, :]], axis=1
    )


def panel_rows(colour, m):
    return PIECE if m < colour else PANEL


def layout(colour, colours):
    panels, pieces = {}, {}
    row = 0
    for place in (1, 3):
        for m in children_of(sources_of(colour)[place]):
            panels[place, m] = (0, row)
            row += panel_rows(colour, m)
    for key in message_keys(colour, 1, colours):
        pieces[1, key] = (0, row)
        row += PIECE
    sizes = [row]
    row = 0
    for place in (2, 3):
        for m in children_of(sources_of(colour)[place]):
            if place == 2:
                panels[place, m] = (1, row)
                row += panel_rows(colour, m)
        if place == 3:
            break
        for key in message_keys(colour, 2, colours):
            pieces[2, key] = (1, row)
            row += PIECE
    own = row
    (m,) = children_of(sources_of(colour)[3])
    forwarded = [(panels[3, m][1], panel_rows(colour, m))]
    panels[3, m] = (1, row)
    row += panel_rows(colour, m)
    offset = offsets_of(colour)[2]
    for key in message_keys(colour, 3, colours):
        here = (moved(key[0], offset), moved(key[1], offset))
        forwarded.append((pieces[1, here][1], PIECE))
        pieces[3, key] = (1, row)
        row += PIECE
    sizes.append(row)
    return panels, pieces, sizes, own, forwarded


def load_piece(ref, row):
    tail = ref[row + SLOTS : row + PIECE, :]
    width = SLOTS - 128
    rest = jnp.concatenate([tail[:, width * i : width * (i + 1)] for i in range(4)], axis=0)
    return jnp.concatenate([ref[row : row + SLOTS, :], rest], axis=1)


def split(value):
    high = value.astype(BF16)
    return high, (value - high.astype(F32)).astype(BF16)


def dot3(left, right, dims):
    lh, ll = left
    rh, rl = right
    dot = functools.partial(
        lax.dot_general, dimension_numbers=dims, preferred_element_type=F32
    )
    return dot(lh, rh) + (dot(lh, rl) + dot(ll, rh))


def shape(*dims):
    return jax.ShapeDtypeStruct(dims, F32)


def call(kernel, outs, args, flops, scratch=(), in_specs=None, **extra):
    vmem = pl.BlockSpec(memory_space=pltpu.VMEM)
    traffic = sum(4 * a.size for a in list(args) + list(outs))
    return pl.pallas_call(
        kernel,
        out_shape=outs,
        in_specs=in_specs or [vmem] * len(args),
        out_specs=[vmem] * len(outs),
        scratch_shapes=list(scratch),
        compiler_params=pltpu.CompilerParams(vmem_limit_bytes=VMEM_LIMIT),
        cost_estimate=pl.CostEstimate(flops=flops, bytes_accessed=traffic, transcendentals=0),
        **extra,
    )(*args)


SMEM = pl.BlockSpec(memory_space=pltpu.SMEM)
VMEM = pl.BlockSpec(memory_space=pltpu.VMEM)


def prep_kernel(colour, red_ref, near_ref, interp_ref, *outs):
    row, col = BOXES[colour]
    own_ref, col_ref, row_ref, r_ref, m_ref, base_ref = outs
    lines = {1: [col_ref, 0], 2: [row_ref, 0]}
    red = red_ref[colour]
    rows = lax.broadcasted_iota(jnp.int32, (SLOTS, SLOTS), 0)
    cols = lax.broadcasted_iota(jnp.int32, (SLOTS, SLOTS), 1)
    for number, (other_row, other_col) in enumerate(BOXES):
        block = near_ref[0, 0, other_row - row + 1, other_col - col + 1]
        kept = (rows + LOW >= red) & (cols + LOW >= red_ref[number])
        base_ref[:, number * SLOTS : (number + 1) * SLOTS] = jnp.where(
            kept, block[LOW:, LOW:], 0.0
        )
    masked = jnp.where((rows < red) & (cols + LOW >= red), interp_ref[0, 0], 0.0)
    rows = lax.broadcasted_iota(jnp.int32, (SLOTS, PTS), 0)
    cols = lax.broadcasted_iota(jnp.int32, (SLOTS, PTS), 1)
    wide = jnp.concatenate([jnp.zeros((SLOTS, LOW), F32), masked], axis=1)
    wide = jnp.where((rows == cols) & (rows < red), 1.0, 0.0) - wide
    r_ref[...] = wide
    compress = split(wide)
    for place in (0, 1, 3, 2):
        offset, source = offsets_of(colour)[place], sources_of(colour)[place]
        for at, m in enumerate(children_of(source)):
            target = (BOXES[m][0] - 2 * offset[0], BOXES[m][1] - 2 * offset[1])
            step_row, step_col = target[0] - row, target[1] - col
            block = split(near_ref[0, 0, step_row + 1, step_col + 1])
            value = dot3(compress, block, NN)
            if place:
                line = lines[2 if place == 2 else 1]
                store_panel(line[0], line[1], value, panel_rows(colour, m))
                line[1] += panel_rows(colour, m)
            else:
                own_ref[at] = value
            if (step_row, step_col) == (0, 0):
                centre = split(value)
                m_ref[...] = 0.5 * (
                    dot3(centre, compress, NT) + dot3(compress, centre, NT)
                )


def prep(colour, red, near, interp):
    row, col = BOXES[colour]
    _, _, sizes, own, _ = layout(colour, ())
    outs = [shape(4, SLOTS, PTS), shape(sizes[0], 128), shape(own, 128)]
    outs += [shape(SLOTS, PTS), shape(SLOTS, SLOTS), shape(SLOTS, 4 * SLOTS)]
    whole = [pl.BlockSpec(o.shape, lambda i, n=len(o.shape): (0,) * n) for o in outs]
    return pl.pallas_call(
        functools.partial(prep_kernel, colour),
        grid=(1,),
        out_shape=outs,
        in_specs=[
            SMEM,
            pl.BlockSpec((1, 1, 3, 3, PTS, PTS), lambda i: (row, col, 0, 0, 0, 0)),
            pl.BlockSpec((1, 1, SLOTS, SLOTS), lambda i: (row, col, 0, 0)),
        ],
        out_specs=whole,
        compiler_params=pltpu.CompilerParams(vmem_limit_bytes=PREP_VMEM_LIMIT),
        cost_estimate=pl.CostEstimate(
            flops=9 * 6 * SLOTS * PTS * PTS, bytes_accessed=4 * 2**20, transcendentals=0
        ),
    )(red, near, interp)


def eliminate(start, out_ref, left_ref, right_ref):
    left_ref[...] = start[:, :128]
    right_ref[:, : SLOTS - 128] = start[:, 128:]
    right_ref[:, SLOTS - 128 :] = jnp.zeros((SLOTS, 256 - SLOTS), F32)
    sub = lax.broadcasted_iota(jnp.int32, (8, 128), 0)
    lane = lax.broadcasted_iota(jnp.int32, (8, 128), 1)
    full = (8, 128)
    tiles = (left_ref, right_ref)
    for group in range(GROUPS):
        at = slice(8 * group, 8 * group + 8)
        tile, first = (0, 8 * group) if group < 16 else (1, 8 * group - 128)
        held = [ref[at, :] for ref in tiles]
        x = [
            jnp.broadcast_to(held[tile][:, first + s : first + s + 1], full) for s in range(8)
        ]
        low = [jnp.zeros(full, F32) for _ in range(8)]
        for j in range(8):
            here = sub == j
            pivot = jnp.broadcast_to(x[j][j : j + 1, :], full)
            inverse = 1.0 / pivot
            root = lax.rsqrt(pivot)
            scaled = x[j] * inverse
            new = []
            for s in range(8):
                if s == j:
                    new.append(jnp.where(here, inverse, -scaled))
                    low[s] = jnp.where(here, root, low[s])
                else:
                    line = jnp.broadcast_to(x[s][j : j + 1, :], full)
                    new.append(jnp.where(here, line * inverse, x[s] - scaled * line))
                    if s < j:
                        low[s] = jnp.where(here, line * root, low[s])
            x = new
        block = (lane >= first) & (lane < first + 8)
        held[tile] = jnp.where(block, jnp.where(lane - first == sub, 1.0, 0.0), held[tile])
        solved, factor = [], []
        for value in held:
            lines = [jnp.broadcast_to(value[s : s + 1, :], full) for s in range(8)]
            solved.append(sum(x[s] * lines[s] for s in range(8)))
            factor.append(sum(low[s] * lines[s] for s in range(8)))
        factor[tile] = jnp.where(lane < first + 8, factor[tile], 0.0)
        out_ref[at, :128] = factor[0]
        out_ref[at, 128:] = (factor[1] if tile else jnp.zeros(full, F32))[:, : SLOTS - 128]
        lines = [
            [jnp.broadcast_to(value[s : s + 1, :], full) for s in range(8)] for value in solved
        ]
        for later in range(group + 1, GROUPS):
            place = slice(8 * later, 8 * later + 8)
            now = [ref[place, :] for ref in tiles]
            column = [
                jnp.broadcast_to(now[tile][:, first + s : first + s + 1], full)
                for s in range(8)
            ]
            now[tile] = jnp.where(block, 0.0, now[tile])
            for number, ref in enumerate(tiles):
                ref[place, :] = now[number] - sum(
                    column[s] * lines[number][s] for s in range(8)
                )


def factor_kernel(colour, keys, red_ref, m_ref, *refs):
    ut_ref = refs[0] if colour else None
    out_ref, *message_refs, left_ref, right_ref = refs[1:] if colour else refs
    red = red_ref[colour]
    rows = lax.broadcasted_iota(jnp.int32, (SLOTS, SLOTS), 0)
    cols = lax.broadcasted_iota(jnp.int32, (SLOTS, SLOTS), 1)
    eye = jnp.where(rows == cols, 1.0, 0.0)
    start = jnp.where((rows < red) & (cols < red), m_ref[...], eye)
    for place, ref in enumerate(message_refs, 1):
        for i, key in enumerate(sent_keys(colour, place, [colour - 1]) if colour else ()):
            store_piece(ref, FACTOR + PIECE * i, ut_ref[keys.index(key)])
    eliminate(start, out_ref, left_ref, right_ref)
    for ref in message_refs:
        store_factor(ref, 0, out_ref[...])


def factor(colour, red, m, ut):
    scratch = [pltpu.VMEM((SLOTS, 128), F32), pltpu.VMEM((SLOTS, 128), F32)]
    before = [colour - 1] if colour else []
    sizes = [FACTOR + PIECE * len(sent_keys(colour, place, before)) for place in (1, 2, 3)]
    args = [red, m] + ([ut] if colour else [])
    return call(
        functools.partial(factor_kernel, colour, local_keys(colour - 1) if colour else ()),
        [shape(SLOTS, SLOTS)] + [shape(n, 128) for n in sizes],
        args,
        flops=8 * 10**9,
        scratch=scratch,
        in_specs=[SMEM] + [VMEM] * (len(args) - 1),
    )


class Pieces:
    def __init__(self, make):
        self.make, self.held = make, {}

    def __getitem__(self, key):
        if key not in self.held:
            self.held[key] = split(self.make(key))
        return self.held[key]


def early_kernel(later, *refs):
    colours = range(later - 1)
    own_ref, *message_refs = refs[:3]
    refs = refs[3:]
    panels, spots, *_ = layout(later, colours)
    ut_refs, w_refs = refs[: later - 1], refs[later - 1 : 2 * (later - 1)]
    outs = refs[2 * (later - 1) :]
    panel_of = {}
    for c in colours:
        for i, (b, m) in enumerate(pairs_of(c)):
            panel_of[b, m] = (c, i)
    colour_of = {b: c for c in colours for b in sources_of(c)}
    w = Pieces(lambda key: w_refs[panel_of[key][0]][panel_of[key][1]])
    for place, box in enumerate(sources_of(later)):
        children = children_of(box)
        if place:
            u = Pieces(
                lambda key: load_piece(message_refs[spots[place, key][0]], spots[place, key][1])
            )
        else:
            u = Pieces(
                lambda key: ut_refs[colour_of[key[0]]][local_keys(colour_of[key[0]]).index(key)]
            )
        for at, m in enumerate(children):
            if place:
                side, row = panels[place, m]
                total = load_panel(message_refs[side], row, panel_rows(later, m))
            else:
                total = own_ref[at]
            for c in colours:
                for t in update_terms(later, c):
                    if t[:2] == (place, m):
                        total = total - dot3(u[t[2:]], w[t[2], m], NN)
            outs[place][at] = total


def early(later, own, messages, uts, ws):
    colours = range(later - 1)
    args = [own, *messages, *[uts[c] for c in colours], *[ws[c] for c in colours]]
    terms = sum(len(update_terms(later, c)) for c in colours)
    return call(
        functools.partial(early_kernel, later),
        [shape(n, SLOTS, PTS) for n in (4, 2, 2, 1)],
        args,
        flops=terms * 6 * SLOTS * SLOTS * PTS,
    )


def stage_kernel(colour, red_ref, *refs):
    later = later_boxes(colour)
    far = colour + 2
    refs = list(refs)

    def take(count):
        taken, refs[:] = refs[:count], refs[count:]
        return taken

    (inverse_ref,) = take(1)
    message_refs = take(3)
    z_refs = take(4 if colour > 1 else 3)
    panels = layout(colour, ())[0]
    if colour:
        before_w, before_ut = take(2)
    r_refs, m_refs = take(len(later)), take(len(later))
    y_refs = take(2) if far < 4 else []
    old_refs = take(colour) if far < 4 else []
    (v_ref,) = take(1)
    if later:
        w_ref, ut_ref = take(2)
    m_outs = take(len(later))
    send_refs = take(2) if far < 4 else []

    red = red_ref[colour]
    cols = lax.broadcasted_iota(jnp.int32, (SLOTS, PTS), 1)
    slots = lax.broadcasted_iota(jnp.int32, (SLOTS, SLOTS), 1)
    v_ref[...] = jnp.zeros(v_ref.shape, F32)
    keys = local_keys(colour)
    parts = {}
    if colour:
        before = pairs_of(colour - 1)
        own_keys = local_keys(colour - 1)
        old_w = Pieces(lambda key: before_w[before.index(key)])
    number = 0
    for place, source in enumerate(sources_of(colour)):
        if place:
            ref = message_refs[place - 1]
            inverse = split(load_factor(ref, 0))
            names = message_keys(colour, place, [colour - 1]) if colour else []
            u = Pieces(lambda key: load_piece(ref, FACTOR + PIECE * names.index(key)))
        else:
            inverse = split(inverse_ref[...])
            u = Pieces(lambda key: before_ut[own_keys.index(key)])
        for at, m in enumerate(children_of(source)):
            if colour > 1 or not place:
                value = z_refs[place][at]
            else:
                side, row = panels[place, m]
                value = load_panel(z_refs[1 + side], row, panel_rows(colour, m))
            for t in update_terms(colour, colour - 1) if colour else ():
                if t[:2] == (place, m):
                    value = value - dot3(u[t[2:]], old_w[t[2], m], NN)
            value = dot3(inverse, split(value), NN)
            if source == BOXES[m]:
                value = jnp.where(cols >= red, value, 0.0)
            v_ref[place * SLOTS : (place + 1) * SLOTS, m * SLOTS : (m + 1) * SLOTS] = jnp.where(
                slots + LOW >= red_ref[m], value[:, LOW:], 0.0
            )
            if later:
                w_ref[number] = value
                number += 1
            if m > colour:
                parts[(source, BOXES[m])] = split(value)
    made = {}
    for n, r_ref, m_ref, m_out in zip(later, r_refs, m_refs, m_outs):
        compress = split(r_ref[...])
        total = m_ref[...]
        for source in sources_of(colour):
            key = (source, BOXES[n])
            if key not in keys:
                continue
            value = dot3(compress, parts[key], NT)
            ut_ref[keys.index(key)] = value
            made[key] = value
            pieces = split(value)
            total = total - dot3(pieces, pieces, NT)
        m_out[...] = total
    for place, (y_ref, ref) in enumerate(zip(y_refs, send_refs), 1):
        row = y_ref.shape[0]
        ref[:row, :] = y_ref[...]
        for key in sent_keys(far, place, range(far - 1)):
            if key in made:
                value = made[key]
            else:
                (c,) = [c for c in range(colour) if key in local_keys(c)]
                value = old_refs[c][local_keys(c).index(key)]
            store_piece(ref, row, value)
            row += PIECE


def stage(colour, red, inverse, messages, z, before, compressors, ms, y, uts):
    later = later_boxes(colour)
    far = colour + 2
    args = [red, inverse, *messages, *z, *before]
    args += [compressors[n] for n in later] + [ms[n] for n in later]
    outs = [shape(4 * SLOTS, 4 * SLOTS)]
    if later:
        outs += [shape(9, SLOTS, PTS), shape(len(local_keys(colour)), SLOTS, SLOTS)]
        outs += [shape(SLOTS, SLOTS)] * len(later)
    if far < 4:
        args += y[far][1:] + [uts[c] for c in range(colour)]
        _, _, sizes, own, _ = layout(far, range(far - 1))
        outs += [shape(sizes[0], 128), shape(own, 128)]
    got = call(
        functools.partial(stage_kernel, colour),
        outs,
        args,
        flops=25 * 6 * SLOTS * SLOTS * PTS,
        in_specs=[SMEM] + [VMEM] * (len(args) - 1),
    )
    v, got = got[0], got[1:]
    if not later:
        return v, None, None, {}, []
    w, ut, got = got[0], got[1], got[2:]
    return v, w, ut, dict(zip(later, got)), got[len(later) :]


TILES = 4 * SLOTS // 128
TRIANGLE = [(i, j) for i in range(TILES) for j in range(i, TILES)]


def gather_kernel(first, v_ref, *refs):
    out_ref = refs[-1]
    high, low = split(v_ref[...])
    for i in range(TILES):
        rows = slice(128 * i, 128 * i + 128)
        value = dot3(
            (high[:, rows], low[:, rows]), (high[:, 128 * i :], low[:, 128 * i :]), TN
        )
        for j in range(i, TILES):
            at = 128 * TRIANGLE.index((i, j))
            block = value[:, 128 * (j - i) : 128 * (j - i) + 128]
            if not first:
                block = block + refs[0][at : at + 128, :]
            out_ref[at : at + 128, :] = block


def gather(v, total=None):
    first = total is None
    return call(
        functools.partial(gather_kernel, first),
        [shape(128 * len(TRIANGLE), 128)],
        [v] if first else [v, total],
        flops=6 * (4 * SLOTS) ** 3,
        **({} if first else {"input_output_aliases": {1: 0}}),
    )[0]


def finish_kernel(flip_ref, base_ref, other_ref, mine_ref, theirs_ref, out_ref):
    swap = flip_ref[1] == 1
    pick = lambda at: jnp.where(swap, other_ref[at], base_ref[at])
    for number, (i, j) in enumerate(TRIANGLE):
        at = slice(128 * number, 128 * number + 128)
        block = jnp.where(swap, theirs_ref[at, :], mine_ref[at, :])
        rows, cols = slice(128 * i, 128 * i + 128), slice(128 * j, 128 * j + 128)
        out_ref[rows, cols] = pick((rows, cols)) - block
        if i != j:
            out_ref[cols, rows] = pick((cols, rows)) - block.T


def finish(flip, base, other, mine, theirs):
    return call(
        finish_kernel,
        [shape(4 * SLOTS, 4 * SLOTS)],
        [flip, base, other, mine, theirs],
        flops=(4 * SLOTS) ** 2,
        in_specs=[SMEM, VMEM, VMEM, VMEM, VMEM],
    )[0]


def fetch(value, offset):
    rows, cols = lax.axis_size("row"), lax.axis_size("col")
    pairs = []
    for i in range(rows):
        for j in range(cols):
            a, b = i + offset[0], j + offset[1]
            if 0 <= a < rows and 0 <= b < cols:
                pairs.append((a * cols + b, i * cols + j))
    return lax.ppermute(value, ("row", "col"), pairs)


def from_partner(value, axis):
    pairs = [(source, source ^ 1) for source in range(lax.axis_size(axis))]
    return lax.ppermute(value, axis, pairs)


def after(value, *others):
    return lax.optimization_barrier((value, *others))[0]


def local(near, interp, red_count, owner_flip):
    red = red_count.reshape(4)
    y, compressors, ms, uts, ws = {}, {}, {}, {}, {}

    def fetch_all(values, colour):
        return [fetch(value, o) for value, o in zip(values, offsets_of(colour)[1:])]

    def prepare(colour, red):
        *y[colour], compressors[colour], ms[colour], base[colour] = prep(
            colour, red, near, interp
        )

    def forward(colour, colours, got, own):
        pieces = [got[row : row + rows] for row, rows in layout(colour, colours)[4]]
        return jnp.concatenate([own, *pieces], axis=0)

    base = {}
    prepare(0, red)
    arrived = {0: [fetch(y[0][1], offsets_of(0)[1])]}
    prepare(1, red)
    arrived[1] = [fetch(y[1][1], offsets_of(1)[1])]
    flip = owner_flip[0, 0]
    total = None
    for c in range(4):
        tied = red if c else after(red, compressors[1])
        inverse, *messages = factor(c, tied, ms[c], uts.get(c - 1))
        late = fetch_all(messages, c)
        if c == 0:
            got = [after(arrived[n][0], inverse) for n in (0, 1)]
            both = [forward(n, (), got[n], y[n][2]) for n in (0, 1)]
            cut = both[0].shape[0]
            both = fetch(jnp.concatenate(both, axis=0), offsets_of(0)[2])
            arrived[0].append(both[:cut])
            arrived[1].append(both[cut:])
            tied = after(red, inverse)
            prepare(2, tied)
            prepare(3, tied)
        if c > 1:
            z = early(c, y[c][0], arrived[c], uts, ws)
        else:
            z = [y[c][0], *arrived[c]]
        if c:
            total = gather(v, total)
        before = [ws[c - 1], uts[c - 1]] if c else []
        tied = red
        if c == 1:
            tied = after(red, start)
        if c == 3:
            tied = after(red, other)
        v, ws[c], uts[c], new, sends = stage(
            c, tied, inverse, late, z, before, compressors, ms, y, uts
        )
        ms.update(new)
        if sends:
            far, known = c + 2, range(c + 1)
            got = fetch(sends[0], offsets_of(far)[1])
            row = forward(far, known, got, sends[1])
            arrived[far] = [got, fetch(row, offsets_of(far)[2])]
        if c == 0:
            start = jnp.concatenate([base[n] for n in range(4)], axis=0)
            start = after(start, v)
            start = jnp.where(flip[0] == 1, from_partner(start, "row"), start)
        if c == 1:
            other = from_partner(start, "col")
    total = gather(v, total)
    total = jnp.where(flip[0] == 1, from_partner(total, "row"), total)
    return finish(flip, start, other, total, from_partner(total, "col"))[None, None]


def solution(mesh):
    in_specs = (
        P("row", "col", None, None, None, None),
        P("row", "col", None, None),
        P("row", "col"),
        P("row", "col", None),
    )
    out_specs = P("row", "col", None, None)
    return jax.shard_map(local, mesh=mesh, in_specs=in_specs, out_specs=out_specs, check_vma=False)
```

```python
import functools

import jax
import jax.numpy as jnp
from jax import lax
from jax.experimental import pallas as pl
from jax.experimental.pallas import tpu as pltpu
from jax.sharding import PartitionSpec as P

BOXES = ((0, 0), (0, 1), (1, 0), (1, 1))
PTS = 256
SLOTS = 160
LOW = 96
GROUPS = SLOTS // 8
VMEM_LIMIT = 24 * 2**20
PREP_VMEM_LIMIT = 48 * 2**20
F32 = jnp.float32
BF16 = jnp.bfloat16
NN = (((1,), (0,)), ((), ()))
NT = (((1,), (1,)), ((), ()))
TN = (((0,), (0,)), ((), ()))


def near_each_other(a, b):
    return abs(a[0] - b[0]) <= 1 and abs(a[1] - b[1]) <= 1


def offsets_of(colour):
    row, col = BOXES[colour]
    step_row, step_col = 1 - 2 * row, 1 - 2 * col
    return ((0, 0), (0, step_col), (step_row, 0), (step_row, step_col))


def sources_of(colour):
    row, col = BOXES[colour]
    return [(row + 2 * dr, col + 2 * dc) for dr, dc in offsets_of(colour)]


def children_of(box):
    return [m for m in range(4) if near_each_other(BOXES[m], box)]


def moved(box, offset):
    return (box[0] - 2 * offset[0], box[1] - 2 * offset[1])


def pairs_of(colour):
    return [(b, m) for b in sources_of(colour) for m in children_of(b)]


def later_boxes(colour):
    return list(range(colour + 1, 4))


def local_keys(colour):
    return [
        (b, BOXES[n]) for n in later_boxes(colour) for b in sources_of(colour)
        if near_each_other(b, BOXES[n])
    ]


def update_terms(later, colour):
    terms = []
    for place, box in enumerate(sources_of(later)):
        for m in children_of(box):
            for b in sources_of(colour):
                if near_each_other(b, box) and near_each_other(b, BOXES[m]):
                    terms.append((place, m, b, box))
    return terms


def message_keys(later, place, colours):
    found = []
    for colour in colours:
        for at, _, b, box in update_terms(later, colour):
            if at == place and (b, box) not in found:
                found.append((b, box))
    return found


def sent_keys(later, place, colours):
    offset = offsets_of(later)[place]
    return [(moved(b, offset), moved(n, offset)) for b, n in message_keys(later, place, colours)]


PIECE = SLOTS * SLOTS // 128
PANEL = SLOTS * PTS // 128
TAIL = PIECE - SLOTS


def pack(value):
    rest = value[:, 128:]
    return value[:, :128], jnp.concatenate(
        [rest[TAIL * i : TAIL * (i + 1)] for i in range(4)], axis=1
    )


def store_piece(ref, row, value):
    head, tail = pack(value)
    ref[row : row + SLOTS, :] = head
    ref[row + SLOTS : row + PIECE, :] = tail


FACTOR = PIECE - 64


def store_factor(ref, row, value):
    last = value[128:, :128]
    block = jnp.concatenate([last[:, :64], last[:, 64:]], axis=0)
    ref[row : row + 64, :] = jnp.concatenate([value[:64, :64], block], axis=1)
    ref[row + 64 : row + 128, :] = value[64:128, :128]
    rest = value[128:, 128:]
    ref[row + 128 : row + FACTOR, :] = jnp.concatenate(
        [rest[8 * i : 8 * i + 8] for i in range(4)], axis=1
    )


def load_factor(ref, row):
    first = ref[row : row + 64, :]
    block = first[:, 64:]
    last = jnp.concatenate([block[:32], block[32:]], axis=1)
    lane = lax.broadcasted_iota(jnp.int32, first.shape, 1)
    first = jnp.where(lane < 64, first, 0.0)
    left = jnp.concatenate([first, ref[row + 64 : row + 128, :], last], axis=0)
    tail = ref[row + 128 : row + FACTOR, :]
    rest = jnp.concatenate([tail[:, 32 * i : 32 * i + 32] for i in range(4)], axis=0)
    right = jnp.concatenate([jnp.zeros((128, 32), F32), rest], axis=0)
    return jnp.concatenate([left, right], axis=1)


def store_panel(ref, row, value, rows):
    if rows == PIECE:
        store_piece(ref, row, value[:, LOW:])
    else:
        ref[row : row + SLOTS, :] = value[:, :128]
        ref[row + SLOTS : row + PANEL, :] = value[:, 128:]


def load_panel(ref, row, rows):
    if rows == PIECE:
        return jnp.concatenate([jnp.zeros((SLOTS, LOW), F32), load_piece(ref, row)], axis=1)
    return jnp.concatenate(
        [ref[row : row + SLOTS, :], ref[row + SLOTS : row + PANEL, :]], axis=1
    )


def panel_rows(colour, m):
    return PIECE if m < colour else PANEL


def layout(colour, colours):
    panels, pieces = {}, {}
    row = 0
    for place in (1, 3):
        for m in children_of(sources_of(colour)[place]):
            panels[place, m] = (0, row)
            row += panel_rows(colour, m)
    for key in message_keys(colour, 1, colours):
        pieces[1, key] = (0, row)
        row += PIECE
    sizes = [row]
    row = 0
    for place in (2, 3):
        for m in children_of(sources_of(colour)[place]):
            if place == 2:
                panels[place, m] = (1, row)
                row += panel_rows(colour, m)
        if place == 3:
            break
        for key in message_keys(colour, 2, colours):
            pieces[2, key] = (1, row)
            row += PIECE
    own = row
    (m,) = children_of(sources_of(colour)[3])
    forwarded = [(panels[3, m][1], panel_rows(colour, m))]
    panels[3, m] = (1, row)
    row += panel_rows(colour, m)
    offset = offsets_of(colour)[2]
    for key in message_keys(colour, 3, colours):
        here = (moved(key[0], offset), moved(key[1], offset))
        forwarded.append((pieces[1, here][1], PIECE))
        pieces[3, key] = (1, row)
        row += PIECE
    sizes.append(row)
    return panels, pieces, sizes, own, forwarded


def load_piece(ref, row):
    tail = ref[row + SLOTS : row + PIECE, :]
    width = SLOTS - 128
    rest = jnp.concatenate([tail[:, width * i : width * (i + 1)] for i in range(4)], axis=0)
    return jnp.concatenate([ref[row : row + SLOTS, :], rest], axis=1)


def split(value):
    high = value.astype(BF16)
    return high, (value - high.astype(F32)).astype(BF16)


def dot3(left, right, dims):
    lh, ll = left
    rh, rl = right
    dot = functools.partial(
        lax.dot_general, dimension_numbers=dims, preferred_element_type=F32
    )
    return dot(lh, rh) + (dot(lh, rl) + dot(ll, rh))


def shape(*dims):
    return jax.ShapeDtypeStruct(dims, F32)


def call(kernel, outs, args, flops, scratch=(), in_specs=None, **extra):
    vmem = pl.BlockSpec(memory_space=pltpu.VMEM)
    traffic = sum(4 * a.size for a in list(args) + list(outs))
    return pl.pallas_call(
        kernel,
        out_shape=outs,
        in_specs=in_specs or [vmem] * len(args),
        out_specs=[vmem] * len(outs),
        scratch_shapes=list(scratch),
        compiler_params=pltpu.CompilerParams(vmem_limit_bytes=VMEM_LIMIT),
        cost_estimate=pl.CostEstimate(flops=flops, bytes_accessed=traffic, transcendentals=0),
        **extra,
    )(*args)


SMEM = pl.BlockSpec(memory_space=pltpu.SMEM)
VMEM = pl.BlockSpec(memory_space=pltpu.VMEM)


def prep_kernel(colour, red_ref, near_ref, interp_ref, *outs):
    row, col = BOXES[colour]
    own_ref, col_ref, row_ref, r_ref, m_ref, base_ref = outs
    lines = {1: [col_ref, 0], 2: [row_ref, 0]}
    red = red_ref[colour]
    rows = lax.broadcasted_iota(jnp.int32, (SLOTS, SLOTS), 0)
    cols = lax.broadcasted_iota(jnp.int32, (SLOTS, SLOTS), 1)
    for number, (other_row, other_col) in enumerate(BOXES):
        block = near_ref[0, 0, other_row - row + 1, other_col - col + 1]
        kept = (rows + LOW >= red) & (cols + LOW >= red_ref[number])
        base_ref[:, number * SLOTS : (number + 1) * SLOTS] = jnp.where(
            kept, block[LOW:, LOW:], 0.0
        )
    masked = jnp.where((rows < red) & (cols + LOW >= red), interp_ref[0, 0], 0.0)
    rows = lax.broadcasted_iota(jnp.int32, (SLOTS, PTS), 0)
    cols = lax.broadcasted_iota(jnp.int32, (SLOTS, PTS), 1)
    wide = jnp.concatenate([jnp.zeros((SLOTS, LOW), F32), masked], axis=1)
    wide = jnp.where((rows == cols) & (rows < red), 1.0, 0.0) - wide
    r_ref[...] = wide
    compress = split(wide)
    for place in (0, 1, 3, 2):
        offset, source = offsets_of(colour)[place], sources_of(colour)[place]
        for at, m in enumerate(children_of(source)):
            target = (BOXES[m][0] - 2 * offset[0], BOXES[m][1] - 2 * offset[1])
            step_row, step_col = target[0] - row, target[1] - col
            block = split(near_ref[0, 0, step_row + 1, step_col + 1])
            value = dot3(compress, block, NN)
            if place:
                line = lines[2 if place == 2 else 1]
                store_panel(line[0], line[1], value, panel_rows(colour, m))
                line[1] += panel_rows(colour, m)
            else:
                own_ref[at] = value
            if (step_row, step_col) == (0, 0):
                centre = split(value)
                m_ref[...] = 0.5 * (
                    dot3(centre, compress, NT) + dot3(compress, centre, NT)
                )


def prep(colour, red, near, interp):
    row, col = BOXES[colour]
    _, _, sizes, own, _ = layout(colour, ())
    outs = [shape(4, SLOTS, PTS), shape(sizes[0], 128), shape(own, 128)]
    outs += [shape(SLOTS, PTS), shape(SLOTS, SLOTS), shape(SLOTS, 4 * SLOTS)]
    whole = [pl.BlockSpec(o.shape, lambda i, n=len(o.shape): (0,) * n) for o in outs]
    return pl.pallas_call(
        functools.partial(prep_kernel, colour),
        grid=(1,),
        out_shape=outs,
        in_specs=[
            SMEM,
            pl.BlockSpec((1, 1, 3, 3, PTS, PTS), lambda i: (row, col, 0, 0, 0, 0)),
            pl.BlockSpec((1, 1, SLOTS, SLOTS), lambda i: (row, col, 0, 0)),
        ],
        out_specs=whole,
        compiler_params=pltpu.CompilerParams(vmem_limit_bytes=PREP_VMEM_LIMIT),
        cost_estimate=pl.CostEstimate(
            flops=9 * 6 * SLOTS * PTS * PTS, bytes_accessed=4 * 2**20, transcendentals=0
        ),
    )(red, near, interp)


def eliminate(start, out_ref, left_ref, right_ref):
    left_ref[...] = start[:, :128]
    right_ref[:, : SLOTS - 128] = start[:, 128:]
    right_ref[:, SLOTS - 128 :] = jnp.zeros((SLOTS, 256 - SLOTS), F32)
    sub = lax.broadcasted_iota(jnp.int32, (8, 128), 0)
    lane = lax.broadcasted_iota(jnp.int32, (8, 128), 1)
    full = (8, 128)
    tiles = (left_ref, right_ref)
    for group in range(GROUPS):
        at = slice(8 * group, 8 * group + 8)
        tile, first = (0, 8 * group) if group < 16 else (1, 8 * group - 128)
        held = [ref[at, :] for ref in tiles]
        x = [
            jnp.broadcast_to(held[tile][:, first + s : first + s + 1], full) for s in range(8)
        ]
        low = [jnp.zeros(full, F32) for _ in range(8)]
        for j in range(8):
            here = sub == j
            pivot = jnp.broadcast_to(x[j][j : j + 1, :], full)
            inverse = 1.0 / pivot
            root = lax.rsqrt(pivot)
            scaled = x[j] * inverse
            new = []
            for s in range(8):
                if s == j:
                    new.append(jnp.where(here, inverse, -scaled))
                    low[s] = jnp.where(here, root, low[s])
                else:
                    line = jnp.broadcast_to(x[s][j : j + 1, :], full)
                    new.append(jnp.where(here, line * inverse, x[s] - scaled * line))
                    if s < j:
                        low[s] = jnp.where(here, line * root, low[s])
            x = new
        block = (lane >= first) & (lane < first + 8)
        held[tile] = jnp.where(block, jnp.where(lane - first == sub, 1.0, 0.0), held[tile])
        solved, factor = [], []
        for value in held:
            lines = [jnp.broadcast_to(value[s : s + 1, :], full) for s in range(8)]
            solved.append(sum(x[s] * lines[s] for s in range(8)))
            factor.append(sum(low[s] * lines[s] for s in range(8)))
        factor[tile] = jnp.where(lane < first + 8, factor[tile], 0.0)
        out_ref[at, :128] = factor[0]
        out_ref[at, 128:] = (factor[1] if tile else jnp.zeros(full, F32))[:, : SLOTS - 128]
        lines = [
            [jnp.broadcast_to(value[s : s + 1, :], full) for s in range(8)] for value in solved
        ]
        for later in range(group + 1, GROUPS):
            place = slice(8 * later, 8 * later + 8)
            now = [ref[place, :] for ref in tiles]
            column = [
                jnp.broadcast_to(now[tile][:, first + s : first + s + 1], full)
                for s in range(8)
            ]
            now[tile] = jnp.where(block, 0.0, now[tile])
            for number, ref in enumerate(tiles):
                ref[place, :] = now[number] - sum(
                    column[s] * lines[number][s] for s in range(8)
                )


def factor_kernel(colour, keys, red_ref, m_ref, *refs):
    ut_ref = refs[0] if colour else None
    out_ref, *message_refs, left_ref, right_ref = refs[1:] if colour else refs
    red = red_ref[colour]
    rows = lax.broadcasted_iota(jnp.int32, (SLOTS, SLOTS), 0)
    cols = lax.broadcasted_iota(jnp.int32, (SLOTS, SLOTS), 1)
    eye = jnp.where(rows == cols, 1.0, 0.0)
    start = jnp.where((rows < red) & (cols < red), m_ref[...], eye)
    for place, ref in enumerate(message_refs, 1):
        for i, key in enumerate(sent_keys(colour, place, [colour - 1]) if colour else ()):
            store_piece(ref, FACTOR + PIECE * i, ut_ref[keys.index(key)])
    eliminate(start, out_ref, left_ref, right_ref)
    for ref in message_refs:
        store_factor(ref, 0, out_ref[...])


def factor(colour, red, m, ut):
    scratch = [pltpu.VMEM((SLOTS, 128), F32), pltpu.VMEM((SLOTS, 128), F32)]
    before = [colour - 1] if colour else []
    sizes = [FACTOR + PIECE * len(sent_keys(colour, place, before)) for place in (1, 2, 3)]
    args = [red, m] + ([ut] if colour else [])
    return call(
        functools.partial(factor_kernel, colour, local_keys(colour - 1) if colour else ()),
        [shape(SLOTS, SLOTS)] + [shape(n, 128) for n in sizes],
        args,
        flops=8 * 10**9,
        scratch=scratch,
        in_specs=[SMEM] + [VMEM] * (len(args) - 1),
    )


class Pieces:
    def __init__(self, make):
        self.make, self.held = make, {}

    def __getitem__(self, key):
        if key not in self.held:
            self.held[key] = split(self.make(key))
        return self.held[key]


def early_kernel(later, *refs):
    colours = range(later - 1)
    own_ref, *message_refs = refs[:3]
    refs = refs[3:]
    panels, spots, *_ = layout(later, colours)
    ut_refs, w_refs = refs[: later - 1], refs[later - 1 : 2 * (later - 1)]
    outs = refs[2 * (later - 1) :]
    panel_of = {}
    for c in colours:
        for i, (b, m) in enumerate(pairs_of(c)):
            panel_of[b, m] = (c, i)
    colour_of = {b: c for c in colours for b in sources_of(c)}
    w = Pieces(lambda key: w_refs[panel_of[key][0]][panel_of[key][1]])
    for place, box in enumerate(sources_of(later)):
        children = children_of(box)
        if place:
            u = Pieces(
                lambda key: load_piece(message_refs[spots[place, key][0]], spots[place, key][1])
            )
        else:
            u = Pieces(
                lambda key: ut_refs[colour_of[key[0]]][local_keys(colour_of[key[0]]).index(key)]
            )
        for at, m in enumerate(children):
            if place:
                side, row = panels[place, m]
                total = load_panel(message_refs[side], row, panel_rows(later, m))
            else:
                total = own_ref[at]
            for c in colours:
                for t in update_terms(later, c):
                    if t[:2] == (place, m):
                        total = total - dot3(u[t[2:]], w[t[2], m], NN)
            outs[place][at] = total


def early(later, own, messages, uts, ws):
    colours = range(later - 1)
    args = [own, *messages, *[uts[c] for c in colours], *[ws[c] for c in colours]]
    terms = sum(len(update_terms(later, c)) for c in colours)
    return call(
        functools.partial(early_kernel, later),
        [shape(n, SLOTS, PTS) for n in (4, 2, 2, 1)],
        args,
        flops=terms * 6 * SLOTS * SLOTS * PTS,
    )


def stage_kernel(colour, red_ref, *refs):
    later = later_boxes(colour)
    far = colour + 2
    refs = list(refs)

    def take(count):
        taken, refs[:] = refs[:count], refs[count:]
        return taken

    (inverse_ref,) = take(1)
    message_refs = take(3)
    z_refs = take(4 if colour > 1 else 3)
    panels = layout(colour, ())[0]
    if colour:
        before_w, before_ut = take(2)
    r_refs, m_refs = take(len(later)), take(len(later))
    y_refs = take(2) if far < 4 else []
    old_refs = take(colour) if far < 4 else []
    (v_ref,) = take(1)
    if later:
        w_ref, ut_ref = take(2)
    m_outs = take(len(later))
    send_refs = take(2) if far < 4 else []

    red = red_ref[colour]
    cols = lax.broadcasted_iota(jnp.int32, (SLOTS, PTS), 1)
    slots = lax.broadcasted_iota(jnp.int32, (SLOTS, SLOTS), 1)
    v_ref[...] = jnp.zeros(v_ref.shape, F32)
    keys = local_keys(colour)
    parts = {}
    if colour:
        before = pairs_of(colour - 1)
        own_keys = local_keys(colour - 1)
        old_w = Pieces(lambda key: before_w[before.index(key)])
    number = 0
    for place, source in enumerate(sources_of(colour)):
        if place:
            ref = message_refs[place - 1]
            inverse = split(load_factor(ref, 0))
            names = message_keys(colour, place, [colour - 1]) if colour else []
            u = Pieces(lambda key: load_piece(ref, FACTOR + PIECE * names.index(key)))
        else:
            inverse = split(inverse_ref[...])
            u = Pieces(lambda key: before_ut[own_keys.index(key)])
        for at, m in enumerate(children_of(source)):
            if colour > 1 or not place:
                value = z_refs[place][at]
            else:
                side, row = panels[place, m]
                value = load_panel(z_refs[1 + side], row, panel_rows(colour, m))
            for t in update_terms(colour, colour - 1) if colour else ():
                if t[:2] == (place, m):
                    value = value - dot3(u[t[2:]], old_w[t[2], m], NN)
            value = dot3(inverse, split(value), NN)
            if source == BOXES[m]:
                value = jnp.where(cols >= red, value, 0.0)
            v_ref[place * SLOTS : (place + 1) * SLOTS, m * SLOTS : (m + 1) * SLOTS] = jnp.where(
                slots + LOW >= red_ref[m], value[:, LOW:], 0.0
            )
            if later:
                w_ref[number] = value
                number += 1
            if m > colour:
                parts[(source, BOXES[m])] = split(value)
    made = {}
    for n, r_ref, m_ref, m_out in zip(later, r_refs, m_refs, m_outs):
        compress = split(r_ref[...])
        total = m_ref[...]
        for source in sources_of(colour):
            key = (source, BOXES[n])
            if key not in keys:
                continue
            value = dot3(compress, parts[key], NT)
            ut_ref[keys.index(key)] = value
            made[key] = value
            pieces = split(value)
            total = total - dot3(pieces, pieces, NT)
        m_out[...] = total
    for place, (y_ref, ref) in enumerate(zip(y_refs, send_refs), 1):
        row = y_ref.shape[0]
        ref[:row, :] = y_ref[...]
        for key in sent_keys(far, place, range(far - 1)):
            if key in made:
                value = made[key]
            else:
                (c,) = [c for c in range(colour) if key in local_keys(c)]
                value = old_refs[c][local_keys(c).index(key)]
            store_piece(ref, row, value)
            row += PIECE


def stage(colour, red, inverse, messages, z, before, compressors, ms, y, uts):
    later = later_boxes(colour)
    far = colour + 2
    args = [red, inverse, *messages, *z, *before]
    args += [compressors[n] for n in later] + [ms[n] for n in later]
    outs = [shape(4 * SLOTS, 4 * SLOTS)]
    if later:
        outs += [shape(9, SLOTS, PTS), shape(len(local_keys(colour)), SLOTS, SLOTS)]
        outs += [shape(SLOTS, SLOTS)] * len(later)
    if far < 4:
        args += y[far][1:] + [uts[c] for c in range(colour)]
        _, _, sizes, own, _ = layout(far, range(far - 1))
        outs += [shape(sizes[0], 128), shape(own, 128)]
    got = call(
        functools.partial(stage_kernel, colour),
        outs,
        args,
        flops=25 * 6 * SLOTS * SLOTS * PTS,
        in_specs=[SMEM] + [VMEM] * (len(args) - 1),
    )
    v, got = got[0], got[1:]
    if not later:
        return v, None, None, {}, []
    w, ut, got = got[0], got[1], got[2:]
    return v, w, ut, dict(zip(later, got)), got[len(later) :]


TILES = 4 * SLOTS // 128
TRIANGLE = [(i, j) for i in range(TILES) for j in range(i, TILES)]


def gather_kernel(first, v_ref, *refs):
    out_ref = refs[-1]
    high, low = split(v_ref[...])
    for i in range(TILES):
        rows = slice(128 * i, 128 * i + 128)
        value = dot3(
            (high[:, rows], low[:, rows]), (high[:, 128 * i :], low[:, 128 * i :]), TN
        )
        for j in range(i, TILES):
            at = 128 * TRIANGLE.index((i, j))
            block = value[:, 128 * (j - i) : 128 * (j - i) + 128]
            if not first:
                block = block + refs[0][at : at + 128, :]
            out_ref[at : at + 128, :] = block


def gather(v, total=None):
    first = total is None
    return call(
        functools.partial(gather_kernel, first),
        [shape(128 * len(TRIANGLE), 128)],
        [v] if first else [v, total],
        flops=6 * (4 * SLOTS) ** 3,
        **({} if first else {"input_output_aliases": {1: 0}}),
    )[0]


def finish_kernel(flip_ref, base_ref, other_ref, mine_ref, theirs_ref, out_ref):
    swap = flip_ref[1] == 1
    pick = lambda at: jnp.where(swap, other_ref[at], base_ref[at])
    for number, (i, j) in enumerate(TRIANGLE):
        at = slice(128 * number, 128 * number + 128)
        block = jnp.where(swap, theirs_ref[at, :], mine_ref[at, :])
        rows, cols = slice(128 * i, 128 * i + 128), slice(128 * j, 128 * j + 128)
        out_ref[rows, cols] = pick((rows, cols)) - block
        if i != j:
            out_ref[cols, rows] = pick((cols, rows)) - block.T


def finish(flip, base, other, mine, theirs):
    return call(
        finish_kernel,
        [shape(4 * SLOTS, 4 * SLOTS)],
        [flip, base, other, mine, theirs],
        flops=(4 * SLOTS) ** 2,
        in_specs=[SMEM, VMEM, VMEM, VMEM, VMEM],
    )[0]


def fetch(value, offset):
    rows, cols = lax.axis_size("row"), lax.axis_size("col")
    pairs = []
    for i in range(rows):
        for j in range(cols):
            a, b = i + offset[0], j + offset[1]
            if 0 <= a < rows and 0 <= b < cols:
                pairs.append((a * cols + b, i * cols + j))
    return lax.ppermute(value, ("row", "col"), pairs)


def from_partner(value, axis):
    pairs = [(source, source ^ 1) for source in range(lax.axis_size(axis))]
    return lax.ppermute(value, axis, pairs)


def after(value, *others):
    return lax.optimization_barrier((value, *others))[0]


def local(near, interp, red_count, owner_flip):
    red = red_count.reshape(4)
    y, compressors, ms, uts, ws = {}, {}, {}, {}, {}

    def fetch_all(values, colour):
        return [fetch(value, o) for value, o in zip(values, offsets_of(colour)[1:])]

    def prepare(colour, red):
        *y[colour], compressors[colour], ms[colour], base[colour] = prep(
            colour, red, near, interp
        )

    def forward(colour, colours, got, own):
        pieces = [got[row : row + rows] for row, rows in layout(colour, colours)[4]]
        return jnp.concatenate([own, *pieces], axis=0)

    base = {}
    prepare(0, red)
    arrived = {0: [fetch(y[0][1], offsets_of(0)[1])]}
    prepare(1, red)
    arrived[1] = [fetch(y[1][1], offsets_of(1)[1])]
    flip = owner_flip[0, 0]
    total = None
    for c in range(4):
        tied = red if c else after(red, compressors[1])
        inverse, *messages = factor(c, tied, ms[c], uts.get(c - 1))
        late = fetch_all(messages, c)
        if c == 0:
            got = [after(arrived[n][0], late[0]) for n in (0, 1)]
            both = [forward(n, (), got[n], y[n][2]) for n in (0, 1)]
            cut = both[0].shape[0]
            both = fetch(jnp.concatenate(both, axis=0), offsets_of(0)[2])
            arrived[0].append(both[:cut])
            arrived[1].append(both[cut:])
            tied = after(red, late[0])
            prepare(2, tied)
            prepare(3, tied)
        if c > 1:
            z = early(c, y[c][0], arrived[c], uts, ws)
        else:
            z = [y[c][0], *arrived[c]]
        if c:
            total = gather(v, total)
        before = [ws[c - 1], uts[c - 1]] if c else []
        tied = red
        if c == 1:
            tied = after(red, start)
        if c == 3:
            tied = after(red, other)
        v, ws[c], uts[c], new, sends = stage(
            c, tied, inverse, late, z, before, compressors, ms, y, uts
        )
        ms.update(new)
        if sends:
            far, known = c + 2, range(c + 1)
            got = fetch(sends[0], offsets_of(far)[1])
            row = forward(far, known, got, sends[1])
            arrived[far] = [got, fetch(row, offsets_of(far)[2])]
        if c == 0:
            start = jnp.concatenate([base[n] for n in range(4)], axis=0)
            start = after(start, v)
            start = jnp.where(flip[0] == 1, from_partner(start, "row"), start)
        if c == 1:
            other = from_partner(start, "col")
    total = gather(v, total)
    total = jnp.where(flip[0] == 1, from_partner(total, "row"), total)
    return finish(flip, start, other, total, from_partner(total, "col"))[None, None]


def solution(mesh):
    in_specs = (
        P("row", "col", None, None, None, None),
        P("row", "col", None, None),
        P("row", "col"),
        P("row", "col", None),
    )
    out_specs = P("row", "col", None, None)
    return jax.shard_map(local, mesh=mesh, in_specs=in_specs, out_specs=out_specs, check_vma=False)
```
